128 devices in a mesh: gen: 4 (over y), dec: 32 (over x, z, core).
Axes of the slice: x: 4, y: 4, z: 4, core: 2. Of those that a mesh axis runs over, the one named last changes fastest.
Arguments:
- latent: bfloat16 [3072, 4, 256], P(('gen', 'dec')), may hold values from -6 to 6
- latent_owner: int32 [3072, 1], P(('gen', 'dec')), may hold values from 0 to 3; in each aligned block of 24 rows (0 to 23, 24 to 47, ...) at most 8 rows name the same one
- next_owner: int32 [4096], P(('gen', 'dec')), may hold values from 0 to 31, as said below
- cache_latent: bfloat16 [4096, 2, 256], P(('gen', 'dec')), may hold values from -6 to 6
- cache_act: bfloat16 [4096, 2, 8192], P(('gen', 'dec')), may hold values from -6 to 6
- weight_in: bfloat16 [3, 144, 512], replicated, may hold values from -0.3125 to 0.3125
- bias_in: float32 [512], replicated, may hold values from -3 to 3
- norm_gain: float32 [512], replicated, may hold values from 0.1 to 1.9
- norm_shift: float32 [512], replicated, may hold values from -3 to 3
- weight_mid: bfloat16 [3, 4608, 512], replicated, may hold values from -0.0546875 to 0.0546875
- bias_mid: float32 [512], replicated, may hold values from -3 to 3
Outputs:
- features: bfloat16 [4096, 4, 8192], P(('gen', 'dec'))
- conv_out: bfloat16 [4096, 4, 8192], P(('gen', 'dec'))
- next_latent: bfloat16 [4096, 2, 256], P(('gen', 'dec'))
- next_act: bfloat16 [4096, 2, 8192], P(('gen', 'dec'))
The draws below stay inside these ranges and needn't reach their ends.
Inputs may be any that keep to these rules, and one draw needn't show every extreme that they name: `latent_owner`: among one device's 24 clips at most 8 name the same index of gen, and in some devices exactly 8 do. `next_owner`: one device's 32 decode slots name one index of dec at most 2 times, and every device's slots name some index exactly 2 times; among the devices of one index of gen, every index of dec is named by exactly 32 slots. Slots with live_mask 0 are named too.
All inputs are finite; a program needn't handle non-finite values.
Results may differ from the reference program's by a relative error of at most 0.0051.
Values may be sent and summed in bfloat16 or wider, within the bound.
A program may use at most 320 MiB of HBM per device.

```python
import math
import jax
import jax.numpy as jnp
import numpy as np
from jax import lax

LAT = 16
CH = 512
GROUPS = 32
FR = 4
HT = 4
WT = 4
CELLS = 16
GEN = 24
CAP_L = 8
DSLOTS = 32
CAP_C = 2
CLIPS = 3072
SLOTS_ALL = 4096
N_GEN = 4
N_DEC = 32


def draw_next_owner(key, part):
    pair_count = DSLOTS // CAP_C
    member = jnp.arange(DSLOTS, dtype=jnp.int32)
    group_index = member // CAP_C
    leading = member % CAP_C == 0
    spare = pair_count + group_index
    rows_all = []
    for gen_index in range(N_GEN):
        row_key = jax.random.fold_in(key, 101 + gen_index)
        offsets_all = jax.random.permutation(jax.random.fold_in(row_key, 1), N_DEC).astype(jnp.int32)
        keep_pair = jax.random.randint(jax.random.fold_in(row_key, 2), (pair_count,), 0, 2).astype(jnp.int32).at[0].set(1)
        merged = leading | (keep_pair[group_index] > 0) | (spare >= N_DEC)
        chosen = jnp.where(merged, group_index, spare).astype(jnp.int32)
        offsets = offsets_all[chosen]
        sender_keys = jax.random.split(jax.random.fold_in(row_key, 3), N_DEC)

        def shuffle_one(sender_key):
            return jax.random.permutation(sender_key, DSLOTS).astype(jnp.int32)
        shuffles = jax.vmap(shuffle_one)(sender_keys)
        sender = jnp.arange(N_DEC, dtype=jnp.int32)[:, None]
        rows_all.append(((sender + offsets[shuffles]) % N_DEC).reshape(-1))
    return jnp.concatenate(rows_all).astype(jnp.int32)


def level_of(own_key, extent, cuts, least, largest):
    def one(dim, blocks):
        steps = jax.random.uniform(jax.random.fold_in(jax.random.fold_in(own_key, 6), dim), (blocks,), jnp.float32, least / len(cuts), largest / len(cuts))
        return jnp.repeat(jnp.exp(steps), extent[dim] // blocks).reshape((-1,) + (1,) * (len(extent) - dim - 1))

    factor_of = one(*cuts[0])
    for cut in cuts[1:]:
        factor_of = factor_of * one(*cut)
    return factor_of


def deal_out(stream_key, own, number, rows, number_of, top, bound, slope):
    sequence = jax.random.permutation(stream_key, number_of)
    packed, ordinary = load_shares(number_of, rows * top, bound, slope, True), load_shares(number_of, rows * top, bound, slope, False)
    places = jnp.arange(number_of)

    def named(lengths, turn):
        used = int((lengths > 0).sum())
        fixed = max(1, used // 4)
        moved = fixed + (places - fixed + turn * (used - fixed)) % max(1, number_of - fixed)
        return jnp.zeros((number_of,), jnp.int32).at[sequence[jnp.where(places < fixed, places, moved)]].set(jnp.asarray(lengths, jnp.int32))

    lengths = jnp.where(number % 4 == 0, named(packed, number // 4), named(ordinary, number - number // 4 - 1))
    mixed = jax.random.permutation(jax.random.fold_in(own, 3), number_of)
    giver, taker = mixed[0:number_of // 2 * 2:2], mixed[1:number_of // 2 * 2:2]
    room = jnp.minimum(lengths[giver] - 1, bound - lengths[taker]) // 2
    room = jnp.where((giver == sequence[0]) | (taker == sequence[0]) | (lengths[taker] == 0), 0, jnp.maximum(room, 0))
    moved = jax.random.randint(jax.random.fold_in(own, 4), (number_of // 2,), 0, 1 << 20) % (room + 1)
    lengths = lengths.at[giver].add(-moved).at[taker].add(moved)
    labels = jnp.searchsorted(jnp.cumsum(lengths), jnp.arange(rows * top), side="right").astype(jnp.int32)
    grid = labels.reshape(top, rows).T
    grid = grid[jax.random.permutation(jax.random.fold_in(own, 1), rows)]
    turn = jax.random.randint(jax.random.fold_in(own, 2), (rows, 1), 0, top)
    return jnp.take_along_axis(grid, (jnp.arange(top)[None, :] + turn) % top, axis=1)


def load_shares(number_of, total, limit, slope, full):
    weights = [(1 << 20) // math.isqrt(standing ** slope) + 1 for standing in range(1, number_of + 1)]
    largest = limit if full else min(limit, max(-(-total // number_of), total * weights[0] // sum(weights)))
    least = 1 if total - largest >= number_of - 1 else 0
    given, spare = [largest] + [least] * (number_of - 1), total - largest - least * (number_of - 1)
    while spare > 0:
        candidates = [i for i in range(1, number_of) if given[i] < largest] or [i for i in range(1, number_of) if given[i] < limit]
        whole, left = sum([weights[i] for i in candidates]), spare
        for i in candidates:
            more = min(limit - given[i], max(1, left * weights[i] // whole), spare)
            given[i] = given[i] + more
            spare = spare - more
    return np.array(given)


def normal_values(rng, shape, width, most, cuts=(), kind=jnp.bfloat16):
    drawn = width * jax.random.normal(rng, shape, jnp.float32)
    if cuts:
        drawn = drawn * level_of(rng, shape, cuts, -0.22, 0.18)
    return jnp.clip(drawn, -most, most).astype(kind)


def setup_inputs(seed: int = 0) -> dict:
    seeds = jax.random.split(jax.random.key(seed), 12)
    latent = normal_values(seeds[0], (CLIPS, FR, LAT * CELLS), 1.0, 6.0, ((0, 128),))
    latent_owner_keys = jax.random.split(jax.random.fold_in(seeds[1], 1), CLIPS // GEN)
    latent_owner_turns = jax.random.permutation(jax.random.fold_in(seeds[1], 3), CLIPS // GEN)
    latent_owner = jax.vmap(lambda own, number: deal_out(jax.random.fold_in(seeds[1], 2), own, number, GEN, N_GEN, 1, CAP_L, 1))(latent_owner_keys, latent_owner_turns).reshape((CLIPS, 1))
    next_owner = draw_next_owner(jax.random.fold_in(seeds[11], 71), 0)
    cache_latent = normal_values(seeds[3], (SLOTS_ALL, 2, LAT * CELLS), 1.0, 6.0, ((0, 128),))
    cache_act = normal_values(seeds[4], (SLOTS_ALL, 2, CELLS * CH), 1.0, 6.0, ((0, 128),))
    weight_in = normal_values(seeds[5], (3, 9 * LAT, CH), (27 * LAT) ** -0.5, 0.3125)
    bias_in = normal_values(seeds[6], (CH,), 0.5, 3.0, (), jnp.float32)
    norm_gain = jnp.clip(1.0 + 0.18 * jax.random.normal(seeds[7], (CH,), jnp.float32), 0.1, 1.9)
    norm_shift = normal_values(seeds[8], (CH,), 0.5, 3.0, (), jnp.float32)
    weight_mid = normal_values(seeds[9], (3, 9 * CH, CH), (27 * CH) ** -0.5, 0.0546875)
    bias_mid = normal_values(seeds[10], (CH,), 0.5, 3.0, (), jnp.float32)
    return {"latent": latent, "latent_owner": latent_owner, "next_owner": next_owner, "cache_latent": cache_latent, "cache_act": cache_act, "weight_in": weight_in, "bias_in": bias_in, "norm_gain": norm_gain, "norm_shift": norm_shift, "weight_mid": weight_mid, "bias_mid": bias_mid}


EPSILON = 1e-06

def tap_allowed(row_tap, col_tap):
    cell = jnp.arange(CELLS, dtype=jnp.int32)
    row_at = cell // WT + row_tap - 1
    col_at = cell % WT + col_tap - 1
    return (row_at >= 0) & (row_at < HT) & (col_at >= 0) & (col_at < WT)

def causal_conv(source, weight, bias_row, cells_axis, pattern):
    slot_count = source.shape[0]
    frame_count = source.shape[1] - 2
    channels = weight.shape[1] // 9
    out_width = weight.shape[2]
    margin = WT + 1
    widths = [(0, 0), (0, 0), (0, 0), (0, 0)]
    widths[cells_axis] = (margin, margin)
    padded = jnp.pad(source, widths)
    summed = jnp.zeros((slot_count, frame_count, CELLS, out_width), jnp.float32) + bias_row
    for row_tap in range(3):
        for col_tap in range(3):
            offset = (row_tap - 1) * WT + (col_tap - 1)
            shifted = lax.slice_in_dim(padded, margin + offset, margin + offset + CELLS, axis=cells_axis)
            allowed = tap_allowed(row_tap, col_tap)
            if cells_axis == 2:
                allowed = allowed[None, None, :, None]
            else:
                allowed = allowed[None, None, None, :]
            shifted = jnp.where(allowed, shifted, 0).astype(jnp.float32)
            spatial = row_tap * 3 + col_tap
            for time_tap in range(3):
                taps = weight[time_tap, spatial * channels:(spatial + 1) * channels].astype(jnp.float32)
                summed = summed + jnp.einsum(pattern, shifted[:, time_tap:time_tap + frame_count], taps, precision=lax.Precision.HIGHEST)
    return summed

def group_act(values, gain_row, shift_row):
    slot_count, frame_count = (values.shape[0], values.shape[1])
    grouped = values.astype(jnp.float32).reshape(slot_count, frame_count, CELLS, GROUPS, CH // GROUPS)
    center = lax.optimization_barrier(jnp.mean(grouped, axis=(2, 4), keepdims=True))
    spread = lax.optimization_barrier(jnp.mean(jnp.square(grouped - center), axis=(2, 4), keepdims=True))
    normed = ((grouped - center) * lax.rsqrt(spread + EPSILON)).reshape(values.shape)
    return jax.nn.silu(normed * gain_row + shift_row).astype(jnp.bfloat16)

def reference(latent, latent_owner, next_owner, cache_latent, cache_act, weight_in, bias_in, norm_gain, norm_shift, weight_mid, bias_mid):
    owner_gen = latent_owner[:, 0].astype(jnp.int32)
    device_count = N_GEN * N_DEC
    grouped = owner_gen.reshape(device_count, GEN)
    position = jnp.arange(GEN, dtype=jnp.int32)
    same_target = grouped[:, :, None] == grouped[:, None, :]
    earlier = (position[None, :] < position[:, None])[None]
    rank_index = lax.optimization_barrier(jnp.sum(same_target & earlier, axis=2)).astype(jnp.int32).reshape(CLIPS)
    maker = (jnp.arange(CLIPS, dtype=jnp.int32) // GEN).astype(jnp.int32)
    source_gen = maker // N_DEC
    column = maker % N_DEC
    slot_index = ((owner_gen * N_DEC + column) * DSLOTS + source_gen * CAP_L + rank_index).astype(jnp.int32)
    placed = jnp.zeros((SLOTS_ALL, FR, LAT * CELLS), jnp.bfloat16).at[slot_index].set(latent)
    live_mask = jnp.zeros((SLOTS_ALL,), jnp.int32).at[slot_index].set(1) > 0
    frames_all = jnp.concatenate([cache_latent, placed], axis=1)
    block_count = SLOTS_ALL // DSLOTS

    def decode(pieces):
        frames_block, history_block, live_block = pieces
        live_grid = live_block[:, None, None, None]
        latent_cells = frames_block.reshape(DSLOTS, FR + 2, LAT, CELLS)
        features = jnp.where(live_grid, causal_conv(latent_cells, weight_in, bias_in, 3, 'sfec,eo->sfco'), 0.0).astype(jnp.bfloat16)
        activated = group_act(features, norm_gain, norm_shift)
        history = history_block.reshape(DSLOTS, 2, CELLS, CH)
        conv_out = jnp.where(live_grid, causal_conv(jnp.concatenate([history, activated], axis=1), weight_mid, bias_mid, 2, 'sfce,eo->sfco'), 0.0).astype(jnp.bfloat16)
        act_tail = jnp.where(live_grid, activated[:, FR - 2:], 0).astype(jnp.bfloat16)
        return (features.reshape(DSLOTS, FR, CELLS * CH), conv_out.reshape(DSLOTS, FR, CELLS * CH), act_tail.reshape(DSLOTS, 2, CELLS * CH))
    features, conv_out, act_tail = lax.map(decode, (frames_all.reshape(block_count, DSLOTS, FR + 2, LAT * CELLS), cache_act.reshape(block_count, DSLOTS, 2, CELLS * CH), live_mask.reshape(block_count, DSLOTS)))
    features = features.reshape(SLOTS_ALL, FR, CELLS * CH)
    conv_out = conv_out.reshape(SLOTS_ALL, FR, CELLS * CH)
    act_tail = act_tail.reshape(SLOTS_ALL, 2, CELLS * CH)
    latent_tail = jnp.where(live_mask[:, None, None], frames_all[:, FR:], 0).astype(jnp.bfloat16)
    owner_rows = next_owner.astype(jnp.int32).reshape(N_GEN, N_DEC * DSLOTS)
    sort_order = jnp.argsort(owner_rows, axis=1, stable=True).astype(jnp.int32)
    row_base = (jnp.arange(N_GEN, dtype=jnp.int32) * (N_DEC * DSLOTS)).astype(jnp.int32)
    source_slot = (sort_order + row_base[:, None]).reshape(SLOTS_ALL).astype(jnp.int32)
    return (features, conv_out, latent_tail[source_slot], act_tail[source_slot])
```

```python
import functools

import jax
import jax.numpy as jnp
import numpy as np
from jax import lax
from jax.experimental import pallas as pl
from jax.experimental.pallas import tpu as pltpu
from jax.sharding import PartitionSpec as P

BF = jnp.bfloat16
F32 = jnp.float32
I32 = jnp.int32

N_GEN, N_DEC = 4, 32
GEN, CAP_L, DSLOTS, CAP_C = 24, 8, 32, 2
FR, CELLS, HT, WT, LAT, CH = 4, 16, 4, 4, 16, 512
MSG_A = 48
MSG_B = 16
EPSILON = 1e-06

TAPS = [4, 1, 3, 5, 7, 0, 2, 6, 8]
REST_CELLS = [y * WT + x for y in range(3) for x in range(3)]
PLAIN_CELLS = [c for c in range(CELLS) if c not in REST_CELLS]


def tap_cells(tap):
    dy, dx = tap // 3 - 1, tap % 3 - 1
    pairs = []
    for y in range(HT):
        for x in range(WT):
            if 0 <= y + dy < HT and 0 <= x + dx < WT:
                pairs.append((y * WT + x, (y + dy) * WT + x + dx))
    return pairs


def patch_selectors():
    first = np.zeros((LAT * CELLS, CELLS * 128), np.float32)
    for tap in range(8):
        for cell, source in tap_cells(tap):
            for e in range(LAT):
                first[e * CELLS + source, cell * 128 + tap * LAT + e] = 1
    rest = np.zeros((3 * LAT * CELLS, len(REST_CELLS) * 128), np.float32)
    for cell, source in tap_cells(8):
        at = REST_CELLS.index(cell)
        for a in range(3):
            for e in range(LAT):
                rest[a * 256 + e * CELLS + source, at * 128 + a * LAT + e] = 1
    return jnp.asarray(first, BF), jnp.asarray(rest, BF)


def dot(a, b):
    return jnp.dot(a, b, preferred_element_type=F32)


def iota(shape, dim):
    return lax.broadcasted_iota(I32, shape, dim)


def onehot(mask):
    return jnp.where(mask, 1.0, 0.0).astype(BF)


def ranked_codes(row, length, per, places):
    sub = iota((length, length), 0)
    lane = iota((length, length), 1)
    wide = jnp.broadcast_to(row, (length, length))
    col = jnp.sum(jnp.where(sub == lane, wide, 0.0), axis=1, keepdims=True)
    same = (wide == col) & (lane < sub)
    rank = jnp.sum(jnp.where(same, 1.0, 0.0), axis=1, keepdims=True)
    return col * per + rank


def spread(codes, where_to, length, width):
    hit = iota((length, width), 0) == where_to
    found = jnp.sum(jnp.where(hit, codes + 1.0, 0.0), axis=0, keepdims=True)
    return found - 1.0


def exchange_kernel(
    latent_ref, owner_ref, next_ref, clips_out, next_out,
    send_a, recv_a, send_b, recv_b, sem_sa, sem_ra, sem_sb, sem_rb,
):
    g = lax.axis_index("gen")
    d = lax.axis_index("dec")
    barrier = pltpu.get_barrier_semaphore()

    def greet_gen(i, _):
        pl.semaphore_signal(barrier, inc=1, device_id={"gen": lax.rem(g + i, N_GEN)},
                            device_id_type=pl.DeviceIdType.MESH)
        return 0

    def greet_dec(i, _):
        pl.semaphore_signal(barrier, inc=1, device_id={"dec": lax.rem(d + i, N_DEC)},
                            device_id_type=pl.DeviceIdType.MESH)
        return 0

    lax.fori_loop(1, N_GEN, greet_gen, 0)
    lax.fori_loop(1, N_DEC, greet_dec, 0)

    codes = ranked_codes(owner_ref[...].astype(F32), GEN, CAP_L, N_GEN)
    lane = iota((GEN, 128), 1)
    clip_at = jnp.where(lane < 96, lane // 4, jnp.where(lane < 96 + GEN, lane - 96, -1))
    lanes = spread(codes, clip_at, GEN, 128)
    row = iota((N_GEN * MSG_A, 128), 0)
    col = iota((N_GEN * MSG_A, 128), 1)
    part = row % MSG_A
    kind = part // 8
    want = ((row // MSG_A) * CAP_L + part % 8).astype(F32)
    col_kind = jnp.where(col < 96, col % 4, 4)
    pick = (want == lanes) & (kind == col_kind)
    pick = pick | ((kind == 5) & (col == 127))
    rows = latent_ref[...].reshape(GEN * FR, LAT * CELLS)
    rows = jnp.concatenate([rows, jnp.ones((32, LAT * CELLS), BF)], axis=0)
    send_a[...] = dot(onehot(pick), rows).astype(BF).reshape(send_a.shape)
    recv_a[g] = send_a[g]

    pl.semaphore_wait(barrier, N_GEN - 1 + N_DEC - 1)

    def copy_a(target, landed):
        return pltpu.make_async_remote_copy(
            src_ref=send_a.at[target], dst_ref=recv_a.at[landed],
            send_sem=sem_sa.at[target], recv_sem=sem_ra.at[landed],
            device_id={"gen": target}, device_id_type=pl.DeviceIdType.MESH,
        )

    for i in range(1, N_GEN):
        copy_a(lax.rem(g + i, N_GEN), g).start()

    codes_b = ranked_codes(next_ref[...].astype(F32), DSLOTS, CAP_C, N_DEC)
    lane_b = iota((DSLOTS, N_GEN * MSG_A), 1)
    slot_at = (lane_b // MSG_A) * CAP_L + lane_b % 8
    lanes_b = spread(codes_b, slot_at, DSLOTS, N_GEN * MSG_A)
    row_b = iota((N_DEC * MSG_B, N_GEN * MSG_A), 0)
    col_b = iota((N_DEC * MSG_B, N_GEN * MSG_A), 1)
    want_b = ((row_b // MSG_B) * CAP_C + row_b % 2).astype(F32)
    pick_b = onehot((want_b == lanes_b) & ((row_b % MSG_B) // 2 == (col_b % MSG_A) // 8))

    for i in range(1, N_GEN):
        other = lax.rem(g + i, N_GEN)
        copy_a(other, other).wait_recv()

    got = recv_a[...].reshape(N_GEN * MSG_A, LAT * CELLS)
    send_b[...] = dot(pick_b, got).astype(BF).reshape(send_b.shape)

    def copy_b(target, landed):
        return pltpu.make_async_remote_copy(
            src_ref=send_b.at[target], dst_ref=recv_b.at[landed],
            send_sem=sem_sb.at[target], recv_sem=sem_rb.at[landed],
            device_id={"dec": target}, device_id_type=pl.DeviceIdType.MESH,
        )

    def start_b(i, _):
        copy_b(lax.rem(d + i, N_DEC), d).start()
        return 0

    lax.fori_loop(1, N_DEC, start_b, 0)
    recv_b[d] = send_b[d]
    clips_out[...] = got

    def take_b(i, _):
        other = lax.rem(d + i, N_DEC)
        copy_b(other, other).wait_recv()
        return 0

    lax.fori_loop(1, N_DEC, take_b, 0)
    next_out[...] = recv_b[...].reshape(N_DEC * MSG_B, LAT * CELLS)

    for i in range(1, N_GEN):
        copy_a(lax.rem(g + i, N_GEN), g).wait_send()

    def sent_b(i, _):
        copy_b(lax.rem(d + i, N_DEC), d).wait_send()
        return 0

    lax.fori_loop(1, N_DEC, sent_b, 0)


def exchange(latent, owner_row, next_row):
    vmem = pl.BlockSpec(memory_space=pltpu.VMEM)
    return pl.pallas_call(
        exchange_kernel,
        out_shape=(
            jax.ShapeDtypeStruct((N_GEN * MSG_A, LAT * CELLS), BF),
            jax.ShapeDtypeStruct((N_DEC * MSG_B, LAT * CELLS), BF),
        ),
        in_specs=[vmem] * 3,
        out_specs=(vmem, vmem),
        scratch_shapes=[
            pltpu.VMEM((N_GEN, MSG_A, LAT * CELLS), BF),
            pltpu.VMEM((N_GEN, MSG_A, LAT * CELLS), BF),
            pltpu.VMEM((N_DEC, MSG_B, LAT * CELLS), BF),
            pltpu.VMEM((N_DEC, MSG_B, LAT * CELLS), BF),
            pltpu.SemaphoreType.DMA((N_GEN,)),
            pltpu.SemaphoreType.DMA((N_GEN,)),
            pltpu.SemaphoreType.DMA((N_DEC,)),
            pltpu.SemaphoreType.DMA((N_DEC,)),
        ],
        compiler_params=pltpu.CompilerParams(
            collective_id=0, has_side_effects=True, vmem_limit_bytes=16 << 20
        ),
        name="exchange",
    )(latent, owner_row, next_row)


def group_mean(total, spread_groups):
    high = total.astype(BF)
    left = total - high.astype(F32)
    mid = left.astype(BF)
    low = (left - mid.astype(F32)).astype(BF)
    return dot(high, spread_groups) + dot(mid, spread_groups) + dot(low, spread_groups)


def silu(u):
    half = 0.5 * u
    return half + half * jnp.tanh(half)


def decode_kernel(
    clips_ref, next_ref, cache_lat_ref, w_in_ref, bias_in_ref, gain_ref, shift_ref,
    bias_mid_ref, sel_ref, rest_ref, hist_hbm, w_mid_hbm,
    feat_hbm, conv_hbm, nlat_ref, nact_hbm,
    hist, w_mid, feat, act, trans, sums, mixed, feat_out, nact_out,
    sem_in, sem_w, sem_out,
):
    hist_copy = pltpu.make_async_copy(hist_hbm, hist, sem_in)
    hist_copy.start()
    w_copies = []
    for at, tap in enumerate(TAPS):
        copy = pltpu.make_async_copy(
            w_mid_hbm.at[:, pl.ds(tap * CH, CH), :], w_mid.at[at], sem_w.at[at]
        )
        copy.start()
        w_copies.append(copy)

    bias_in = bias_in_ref[...].reshape(1, CH)
    gain = gain_ref[...].reshape(1, CH)
    shift = shift_ref[...].reshape(1, CH)
    bias_mid = bias_mid_ref[...].reshape(1, CH)
    groups = (iota((CH, CH), 0) // 16) == (iota((CH, CH), 1) // 16)
    groups = jnp.where(groups, 1.0 / 256.0, 0.0).astype(BF)
    w_cat = jnp.concatenate(
        [w_in_ref[a, :128, :] for a in range(3)]
        + [w_in_ref[a, 128:144, :] for a in range(3)]
        + [jnp.zeros((80, CH), BF)],
        axis=0,
    )

    def normalised(read, write, rows):
        total = jnp.zeros((rows, CH), F32)
        for c in range(CELLS):
            total = total + read(c).astype(F32)
        center = group_mean(total, groups)
        square = jnp.zeros((rows, CH), F32)
        for c in range(CELLS):
            off = read(c).astype(F32) - center
            square = square + off * off
        scale = lax.rsqrt(group_mean(square, groups) + EPSILON) * gain
        for c in range(CELLS):
            u = (read(c).astype(F32) - center) * scale + shift
            write(c, silu(u).astype(BF))

    def features_of(frames, rows, write, live):
        shifted = [frames[a * 32:a * 32 + rows] for a in range(3)]
        taps = dot(frames, sel_ref[...]).astype(BF)
        rest = dot(jnp.concatenate(shifted, axis=1), rest_ref[...]).astype(BF)
        for cells, depth in ((REST_CELLS, 512), (PLAIN_CELLS, 384)):
            left = []
            for c in cells:
                block = [taps[a * 32:a * 32 + rows, c * 128:c * 128 + 128] for a in range(3)]
                if depth == 512:
                    at = REST_CELLS.index(c)
                    block.append(rest[:, at * 128:at * 128 + 128])
                left.append(jnp.concatenate(block, axis=1))
            made = dot(jnp.concatenate(left, axis=0), w_cat[:depth])
            for i, c in enumerate(cells):
                write(c, ((made[i * rows:(i + 1) * rows] + bias_in) * live).astype(BF))

    row = iota((320, 256), 0)
    col = iota((320, 256), 1)
    frame, slot = row // 32, row % 32
    clip_row = (slot // 8) * MSG_A + jnp.where(row < 192, frame - 2, 4) * 8 + slot % 8
    source_row = jnp.where(row < 64, 192 + slot * 2 + frame, clip_row)
    stacked = jnp.concatenate([clips_ref[...], cache_lat_ref[...].reshape(64, 256)], axis=0)
    placed = dot(onehot(col == source_row), stacked)
    frames = placed[:192].astype(BF)
    live = jnp.concatenate([placed[192:], placed[192:]], axis=1)

    def put_feat(c, value):
        feat[c] = value

    features_of(frames, 128, put_feat, live)

    def put_act(c, value):
        act[c] = value

    normalised(lambda c: feat[c], put_act, 128)

    hist_copy.wait()
    turn = onehot(iota((64, 64), 1) == (iota((64, 64), 0) % 32) * 2 + iota((64, 64), 0) // 32)
    for c in range(CELLS):
        old = dot(turn, hist[:, :, c * CH:(c + 1) * CH].reshape(64, CH)).astype(BF)
        q = [old[:32], old[32:]] + [act[c, t * 32:t * 32 + 32] for t in range(4)]
        for tile in range(2):
            d0, d1, d2, d3 = q[2 * tile:2 * tile + 4]
            at = slice(tile * 32, tile * 32 + 32)
            trans[0, c, at] = d0 - d2
            trans[1, c, at] = d1 + d2
            trans[2, c, at] = d2 - d1
            trans[3, c, at] = d1 - d3

    order = onehot(
        iota((128, 128), 1) == (iota((128, 128), 0) % 4) * 32 + iota((128, 128), 0) // 4
    )
    for c in range(CELLS):
        turned = dot(order, feat[c]).astype(BF).reshape(32, 4, CH)
        feat_out[:, :, c * CH:(c + 1) * CH] = turned
    feat_copy = pltpu.make_async_copy(feat_out, feat_hbm, sem_out.at[0])
    feat_copy.start()

    flags = lax.dot_general(
        onehot(iota((8, 256), 1) == 0), next_ref[...], (((1,), (1,)), ((), ())),
        preferred_element_type=F32,
    ).astype(BF)
    big = iota((512, 128), 0)
    index = (big // MSG_B) * 2 + big % 2
    filled = dot(flags, onehot(((big % MSG_B) // 2 == 5) & (index == iota((512, 128), 1))))
    before = onehot(iota((128, 128), 0) < iota((128, 128), 1))
    place = dot(filled.astype(BF), before)
    take = (filled[:1] > 0.5) & (place[:1] == iota((32, 128), 0).astype(F32))
    take = onehot(take)
    lane = iota((128, 512), 1)
    lane_index = (lane // MSG_B) * 2 + lane % 2
    entry = lane_index == iota((128, 512), 0)
    picks = [
        dot(take, onehot(entry & ((lane % MSG_B) // 2 == kind))).astype(BF) for kind in range(5)
    ]
    moved = dot(jnp.concatenate(picks, axis=0), next_ref[...])
    later = moved[:128].astype(BF)
    live_next = jnp.concatenate([moved[128:160], moved[128:160]], axis=1)
    live_next = jnp.concatenate([live_next, live_next], axis=0)
    pair = onehot(iota((64, 64), 1) == (iota((64, 64), 0) % 2) * 32 + iota((64, 64), 0) // 2)
    nlat_ref[...] = dot(pair, later[64:]).astype(BF).reshape(32, 2, 256)

    features_of(later, 64, lambda c, value: mixed.__setitem__(c, value), live_next)

    def put_next(c, value):
        value = (value.astype(F32) * live_next).astype(BF)
        nact_out[:, :, c * CH:(c + 1) * CH] = dot(pair, value).astype(BF).reshape(32, 2, CH)

    normalised(lambda c: mixed[c], put_next, 64)
    nact_copy = pltpu.make_async_copy(nact_out, nact_hbm, sem_out.at[1])
    nact_copy.start()

    for at, tap in enumerate(TAPS):
        w_copies[at].wait()
        g0 = w_mid[at, 0].astype(F32)
        g1 = w_mid[at, 1].astype(F32)
        g2 = w_mid[at, 2].astype(F32)
        ends = g0 + g2
        weights = [
            w_mid[at, 0], ((ends + g1) * 0.5).astype(BF), ((ends - g1) * 0.5).astype(BF),
            w_mid[at, 2],
        ]
        pairs = tap_cells(tap)
        for j in range(4):
            left = jnp.concatenate([trans[j, source] for _, source in pairs], axis=0)
            made = dot(left, weights[j])
            for i, (cell, _) in enumerate(pairs):
                piece = made[i * 64:(i + 1) * 64]
                if at == 0:
                    sums[j, cell] = piece
                else:
                    sums[j, cell] += piece

    r128 = iota((128, 128), 0)
    back = onehot(iota((128, 128), 1) == (r128 % 2) * 64 + ((r128 % 4) // 2) * 32 + r128 // 4)
    keep = live[:64]
    feat_copy.wait()
    conv_out = feat_out
    conv_copies = []
    for c in range(CELLS):
        both = sums[1, c] + sums[2, c]
        apart = sums[1, c] - sums[2, c]
        even = ((sums[0, c] + both + bias_mid) * keep).astype(BF)
        odd = ((apart - sums[3, c] + bias_mid) * keep).astype(BF)
        turned = dot(back, jnp.concatenate([even, odd], axis=0)).astype(BF)
        conv_out[:, :, c * CH:(c + 1) * CH] = turned.reshape(32, 4, CH)
        if c % 4 == 3:
            lanes = pl.ds((c - 3) * CH, 4 * CH)
            copy = pltpu.make_async_copy(
                conv_out.at[:, :, lanes], conv_hbm.at[:, :, lanes], sem_out.at[2 + c // 4]
            )
            copy.start()
            conv_copies.append(copy)
    for copy in [nact_copy] + conv_copies:
        copy.wait()


def decode(clips, later, cache_latent, cache_act, weight_in, bias_in, gain, shift,
           weight_mid, bias_mid):
    sel, rest = patch_selectors()
    vmem = pl.BlockSpec(memory_space=pltpu.VMEM)
    hbm = pl.BlockSpec(memory_space=pl.ANY)
    wide = CELLS * CH
    return pl.pallas_call(
        decode_kernel,
        out_shape=(
            jax.ShapeDtypeStruct((DSLOTS, FR, wide), BF),
            jax.ShapeDtypeStruct((DSLOTS, FR, wide), BF),
            jax.ShapeDtypeStruct((DSLOTS, 2, LAT * CELLS), BF),
            jax.ShapeDtypeStruct((DSLOTS, 2, wide), BF),
        ),
        in_specs=[vmem] * 10 + [hbm, hbm],
        out_specs=(hbm, hbm, vmem, hbm),
        scratch_shapes=[
            pltpu.VMEM((DSLOTS, 2, wide), BF),
            pltpu.VMEM((9, 3, CH, CH), BF),
            pltpu.VMEM((CELLS, 128, CH), BF),
            pltpu.VMEM((CELLS, 128, CH), BF),
            pltpu.VMEM((4, CELLS, 64, CH), BF),
            pltpu.VMEM((4, CELLS, 64, CH), F32),
            pltpu.VMEM((CELLS, 64, CH), BF),
            pltpu.VMEM((DSLOTS, FR, wide), BF),
            pltpu.VMEM((DSLOTS, 2, wide), BF),
            pltpu.SemaphoreType.DMA,
            pltpu.SemaphoreType.DMA((9,)),
            pltpu.SemaphoreType.DMA((6,)),
        ],
        compiler_params=pltpu.CompilerParams(vmem_limit_bytes=58 << 20),
        name="decode",
    )(clips, later, cache_latent, weight_in, bias_in, gain, shift, bias_mid, sel, rest,
      cache_act, weight_mid)


def shards(latent, latent_owner, next_owner, cache_latent, cache_act, weight_in, bias_in,
           norm_gain, norm_shift, weight_mid, bias_mid):
    clips, later = exchange(
        latent, latent_owner.reshape(1, GEN), next_owner.reshape(1, DSLOTS)
    )
    return decode(clips, later, cache_latent, cache_act, weight_in, bias_in, norm_gain,
                  norm_shift, weight_mid, bias_mid)


def solution(mesh):
    both = ("gen", "dec")
    in_specs = (
        P(both, None, None), P(both, None), P(both), P(both, None, None), P(both, None, None),
        P(), P(), P(), P(), P(), P(),
    )
    out_specs = (P(both, None, None),) * 4
    return jax.shard_map(shards, mesh=mesh, in_specs=in_specs, out_specs=out_specs, check_vma=False)
```

```python
import functools

import jax
import jax.numpy as jnp
import numpy as np
from jax import lax
from jax.experimental import pallas as pl
from jax.experimental.pallas import tpu as pltpu
from jax.sharding import PartitionSpec as P

BF = jnp.bfloat16
F32 = jnp.float32
I32 = jnp.int32

N_GEN, N_DEC = 4, 32
GEN, CAP_L, DSLOTS, CAP_C = 24, 8, 32, 2
FR, CELLS, HT, WT, LAT, CH = 4, 16, 4, 4, 16, 512
PART = 8
MSG_A = CAP_L * PART
MSG_B = CAP_C * PART
DEAD, EMPTY = 64.0, 128.0
EPSILON = 1e-06

AHEAD = 3
LIM = 65400 << 10
TAPS = [4, 1, 3, 5, 7, 0, 2, 6, 8]
REST_CELLS = [y * WT + x for y in range(3) for x in range(3)]
PLAIN_CELLS = [c for c in range(CELLS) if c not in REST_CELLS]


def tap_cells(tap):
    dy, dx = tap // 3 - 1, tap % 3 - 1
    pairs = []
    for y in range(HT):
        for x in range(WT):
            if 0 <= y + dy < HT and 0 <= x + dx < WT:
                pairs.append((y * WT + x, (y + dy) * WT + x + dx))
    return pairs


def patch_selectors():
    first = np.zeros((LAT * CELLS, CELLS * 128), np.float32)
    for tap in range(8):
        for cell, source in tap_cells(tap):
            for e in range(LAT):
                first[e * CELLS + source, cell * 128 + tap * LAT + e] = 1
    rest = np.zeros((3 * LAT * CELLS, len(REST_CELLS) * 128), np.float32)
    for cell, source in tap_cells(8):
        at = REST_CELLS.index(cell)
        for a in range(3):
            for e in range(LAT):
                rest[a * 256 + e * CELLS + source, at * 128 + a * LAT + e] = 1
    return jnp.asarray(first, BF), jnp.asarray(rest, BF)


def dot(a, b):
    return jnp.dot(a, b, preferred_element_type=F32)


def iota(shape, dim):
    return lax.broadcasted_iota(I32, shape, dim)


def onehot(mask):
    return jnp.where(mask, 1.0, 0.0).astype(BF)


def ranked_codes(row, length, per):
    sub = iota((length, length), 0)
    lane = iota((length, length), 1)
    wide = jnp.broadcast_to(row, (length, length))
    col = jnp.sum(jnp.where(sub == lane, wide, 0.0), axis=1, keepdims=True)
    same = (wide == col) & (lane < sub)
    rank = jnp.sum(jnp.where(same, 1.0, 0.0), axis=1, keepdims=True)
    return col * per + rank


def spread(codes, where_to, length, width):
    hit = iota((length, width), 0) == where_to
    found = jnp.sum(jnp.where(hit, codes + 1.0, 0.0), axis=0, keepdims=True)
    return found - 1.0


def group_mean(total, spread_groups):
    high = total.astype(BF)
    left = total - high.astype(F32)
    mid = left.astype(BF)
    low = (left - mid.astype(F32)).astype(BF)
    return dot(high, spread_groups) + dot(mid, spread_groups) + dot(low, spread_groups)


def silu(u):
    half = 0.5 * u
    return half + half * jnp.tanh(half)


def block_ones():
    same = (iota((CH, CH), 0) // 16) == (iota((CH, CH), 1) // 16)
    return jnp.where(same, 1.0 / 256.0, 0.0).astype(BF)


def input_weights(w_in_ref):
    return jnp.concatenate(
        [w_in_ref[a, :128, :] for a in range(3)]
        + [w_in_ref[a, 128:144, :] for a in range(3)]
        + [jnp.zeros((80, CH), BF)],
        axis=0,
    )


def normalised(read, write, rows, groups, gain, shift):
    total = jnp.zeros((rows, CH), F32)
    for c in range(CELLS):
        total = total + read(c).astype(F32)
    center = group_mean(total, groups)
    square = jnp.zeros((rows, CH), F32)
    for c in range(CELLS):
        off = read(c).astype(F32) - center
        square = square + off * off
    scale = lax.rsqrt(group_mean(square, groups) + EPSILON) * gain
    for c in range(CELLS):
        u = (read(c).astype(F32) - center) * scale + shift
        write(c, silu(u).astype(BF))


def patches(frames, rows, sel, rest):
    shifted = [frames[a * 32:a * 32 + rows] for a in range(3)]
    return (
        dot(frames, sel[...]).astype(BF),
        dot(jnp.concatenate(shifted, axis=1), rest[...]).astype(BF),
    )


def features_of(found, rows, w_cat, bias, live, write, groups):
    taps, rest = found
    for cells in groups:
        depth = 512 if cells[0] in REST_CELLS else 384
        left = []
        for c in cells:
            block = [taps[a * 32:a * 32 + rows, c * 128:c * 128 + 128] for a in range(3)]
            if depth == 512:
                at = REST_CELLS.index(c)
                block.append(rest[:, at * 128:at * 128 + 128])
            left.append(jnp.concatenate(block, axis=1))
        made = dot(jnp.concatenate(left, axis=0), w_cat[:depth])
        for i, c in enumerate(cells):
            write(c, ((made[i * rows:(i + 1) * rows] + bias) * live).astype(BF))


def lane_halves(pick_row, pick_col_of, source):
    return jnp.concatenate(
        [dot(onehot(pick_row == pick_col_of(half)), source) for half in range(2)], axis=1
    )


def front_kernel(
    latent_hbm, owner_hbm, next_hbm, cache_hbm, hist_hbm, w_in_hbm, bias_hbm, gain_hbm,
    shift_hbm, sel_hbm, rest_hbm,
    trans_hbm, feat_hbm, live_hbm, later_hbm,
    latent, owner, nexts, cache, hist, w_in, bias_v, gain_v, shift_v, sel, rest,
    send_a, recv_a, send_b, recv_x, recv_z, recv_c, feat, old, trans, live_v,
    sem_in, sem_out, sem_sa, sem_ra, sem_sx, sem_rx, sem_sz, sem_rz, sem_sc, sem_rc,
):
    g = lax.axis_index("gen")
    d = lax.axis_index("dec")
    x, z, c = d // 8, (d // 2) % 4, d % 2
    gens = [lax.rem(g + i, 4) for i in (1, 2, 3)]
    xs = [lax.rem(x + i, 4) for i in (1, 2, 3)]
    zs = [lax.rem(z + i, 4) for i in (1, 2, 3)]
    mesh_ids = pl.DeviceIdType.MESH
    barrier = pltpu.get_barrier_semaphore()
    peers = [{"gen": p} for p in gens]
    peers += [{"dec": p * 8 + z * 2 + c} for p in xs]
    peers += [{"dec": x * 8 + p * 2 + c} for p in zs]
    peers += [{"dec": x * 8 + z * 2 + (1 - c)}]
    for peer in peers:
        pl.semaphore_signal(barrier, inc=1, device_id=peer, device_id_type=mesh_ids)

    loads = []
    for i, (src, dst) in enumerate((
        (latent_hbm, latent), (owner_hbm, owner), (next_hbm, nexts), (cache_hbm, cache),
        (hist_hbm, hist), (sel_hbm, sel), (rest_hbm, rest), (w_in_hbm, w_in),
        (bias_hbm, bias_v), (gain_hbm, gain_v), (shift_hbm, shift_v),
    )):
        load = pltpu.make_async_copy(src, dst, sem_in.at[i])
        load.start()
        loads.append(load)

    loads[0].wait()
    loads[1].wait()
    loads[2].wait()
    codes = ranked_codes(owner[...].astype(F32), GEN, CAP_L)
    lane = iota((GEN, 256), 1)
    clip_at = jnp.where(lane < 192, (lane % 96) // 4, -1)
    lanes = spread(codes, clip_at, GEN, 256)
    row = iota((N_GEN * MSG_A, 256), 0)
    col = iota((N_GEN * MSG_A, 256), 1)
    named = ((row // MSG_A) * CAP_L + (row % MSG_A) // PART).astype(F32) == lanes
    pick = named & ((row % PART) == (col % 4) * 2 + col // 96) & (col < 192)
    present = jnp.sum(jnp.where(pick, 1.0, 0.0), axis=1, keepdims=True)
    rows = latent[...].reshape(GEN * FR, LAT * CELLS)
    rows = jnp.concatenate([rows[:, :128], rows[:, 128:], jnp.zeros((64, 128), BF)], axis=0)
    ready = jnp.where(present > 0.5, dot(onehot(pick), rows), DEAD)
    send_a[...] = ready.astype(BF).reshape(send_a.shape)
    recv_a[g] = send_a[g]

    pl.semaphore_wait(barrier, len(peers))

    def copy_a(target, landed):
        return pltpu.make_async_remote_copy(
            src_ref=send_a.at[target], dst_ref=recv_a.at[landed],
            send_sem=sem_sa.at[target], recv_sem=sem_ra.at[landed],
            device_id={"gen": target}, device_id_type=mesh_ids,
        )

    for p in gens:
        copy_a(p, g).start()

    codes_b = ranked_codes(nexts[...].astype(F32), DSLOTS, CAP_C)
    lane_b = iota((DSLOTS, 256), 1)
    lanes_b = spread(codes_b, lane_b // PART, DSLOTS, 256)
    row_b = iota((N_DEC * MSG_B, 256), 0)
    col_b = iota((N_DEC * MSG_B, 256), 1)
    pick_b = ((row_b // PART).astype(F32) == lanes_b) & ((row_b % PART) == (col_b % PART))
    filled = jnp.sum(jnp.where(pick_b, 1.0, 0.0), axis=1, keepdims=True)
    pick_b = onehot(pick_b)
    loads[4].wait()
    turn = onehot(iota((64, 64), 1) == (iota((64, 64), 0) % 32) * 2 + iota((64, 64), 0) // 32)
    for cell in range(CELLS):
        lanes_c = slice(cell * CH, (cell + 1) * CH)
        old[cell] = dot(turn, hist[:, :, lanes_c].reshape(64, CH)).astype(BF)
    loads[3].wait()
    for load in loads[5:]:
        load.wait()
    groups = block_ones()
    w_cat = input_weights(w_in)
    bias = bias_v[...].reshape(1, CH)
    gain = gain_v[...].reshape(1, CH)
    shift = shift_v[...].reshape(1, CH)
    cached = dot(turn, cache[...].reshape(64, 256)).astype(BF)

    for p in gens:
        copy_a(p, p).wait_recv()
    got = recv_a[...].reshape(N_GEN * MSG_A, 128)
    messages = jnp.where(filled > 0.5, dot(pick_b, got), EMPTY)
    send_b[...] = messages.astype(BF).reshape(send_b.shape)

    def copy_x(target, landed):
        return pltpu.make_async_remote_copy(
            src_ref=send_b.at[target], dst_ref=recv_x.at[landed],
            send_sem=sem_sx.at[target], recv_sem=sem_rx.at[landed],
            device_id={"dec": target * 8 + z * 2 + c}, device_id_type=mesh_ids,
        )

    def copy_z(target, landed):
        return pltpu.make_async_remote_copy(
            src_ref=recv_x.at[:, target], dst_ref=recv_z.at[landed],
            send_sem=sem_sz.at[target], recv_sem=sem_rz.at[landed],
            device_id={"dec": x * 8 + target * 2 + c}, device_id_type=mesh_ids,
        )

    def copy_c(target, landed):
        return pltpu.make_async_remote_copy(
            src_ref=recv_z.at[:, :, target], dst_ref=recv_c.at[landed],
            send_sem=sem_sc, recv_sem=sem_rc,
            device_id={"dec": x * 8 + z * 2 + target}, device_id_type=mesh_ids,
        )

    for p in xs:
        copy_x(p, x).start()
    recv_x[x] = send_b[x]

    r128 = iota((128, 256), 0)
    placed = lane_halves(
        iota((128, 256), 1), lambda half: (r128 % 32) * PART + (r128 // 32) * 2 + half, got
    )
    live = jnp.where(placed[:, :1] < 32.0, 1.0, 0.0)
    live_v[...] = jnp.broadcast_to(live[:64], (64, 128))
    fresh = jnp.where(placed > 32.0, 0.0, placed).astype(BF)
    found = patches(jnp.concatenate([cached, fresh], axis=0), 128, sel, rest)

    def put_feat(cell, value):
        feat[cell] = value

    features_of(found, 128, w_cat, bias, live, put_feat, (REST_CELLS,))

    for p in xs:
        copy_x(p, p).wait_recv()
    for p in zs:
        copy_z(p, z).start()
    recv_z[z] = recv_x[:, z]

    features_of(found, 128, w_cat, bias, live, put_feat, (PLAIN_CELLS,))
    outs = [pltpu.make_async_copy(feat, feat_hbm, sem_out.at[0]),
            pltpu.make_async_copy(live_v, live_hbm, sem_out.at[1])]
    for out in outs:
        out.start()

    total = jnp.zeros((128, CH), F32)
    for cell in range(CELLS):
        total = total + feat[cell].astype(F32)
    center = group_mean(total, groups)
    square = jnp.zeros((128, CH), F32)
    for cell in range(CELLS):
        off = feat[cell].astype(F32) - center
        square = square + off * off
    scale = lax.rsqrt(group_mean(square, groups) + EPSILON) * gain

    for p in zs:
        copy_z(p, p).wait_recv()
    copy_c(1 - c, c).start()
    recv_c[c] = recv_z[:, :, c]

    for cell in range(CELLS):
        u = (feat[cell].astype(F32) - center) * scale + shift
        act = silu(u).astype(BF)
        q = [old[cell, :32], old[cell, 32:]] + [act[t * 32:t * 32 + 32] for t in range(4)]
        for tile in range(2):
            d0, d1, d2, d3 = q[2 * tile:2 * tile + 4]
            at = slice(tile * 32, tile * 32 + 32)
            trans[0, cell, at] = d0 - d2
            trans[1, cell, at] = d1 + d2
            trans[2, cell, at] = d2 - d1
            trans[3, cell, at] = d1 - d3
        if cell % 4 == 3:
            part = pl.ds(cell - 3, 4)
            out = pltpu.make_async_copy(
                trans.at[:, part], trans_hbm.at[:, part], sem_out.at[2 + cell // 4]
            )
            out.start()
            outs.append(out)

    copy_c(1 - c, 1 - c).wait_recv()
    out = pltpu.make_async_copy(recv_c, later_hbm, sem_out.at[6])
    out.start()
    outs.append(out)
    for p in gens:
        copy_a(p, g).wait_send()
    for p in xs:
        copy_x(p, x).wait_send()
    for p in zs:
        copy_z(p, z).wait_send()
    copy_c(1 - c, c).wait_send()
    for out in outs:
        out.wait()


def front(latent, owner, nexts, cache_latent, cache_act, weight_in, bias_in, gain, shift, sel, rest):
    hbm = pl.BlockSpec(memory_space=pltpu.HBM)
    wide = CELLS * CH
    dma = pltpu.SemaphoreType.DMA
    return pl.pallas_call(
        front_kernel,
        out_shape=(
            jax.ShapeDtypeStruct((4, CELLS, 64, CH), BF),
            jax.ShapeDtypeStruct((CELLS, 128, CH), BF),
            jax.ShapeDtypeStruct((64, 128), F32),
            jax.ShapeDtypeStruct((2, 4, 4, MSG_B, 128), BF),
        ),
        in_specs=[hbm] * 11,
        out_specs=(hbm,) * 4,
        scratch_shapes=[
            pltpu.VMEM((GEN, FR, LAT * CELLS), BF),
            pltpu.VMEM((1, GEN), I32),
            pltpu.VMEM((1, DSLOTS), I32),
            pltpu.VMEM((DSLOTS, 2, LAT * CELLS), BF),
            pltpu.VMEM((DSLOTS, 2, wide), BF),
            pltpu.VMEM((3, 9 * LAT, CH), BF),
            pltpu.VMEM((CH,), F32),
            pltpu.VMEM((CH,), F32),
            pltpu.VMEM((CH,), F32),
            pltpu.VMEM(sel.shape, BF),
            pltpu.VMEM(rest.shape, BF),
            pltpu.VMEM((N_GEN, MSG_A, 128), BF),
            pltpu.VMEM((N_GEN, MSG_A, 128), BF),
            pltpu.VMEM((4, 4, 2, MSG_B, 128), BF),
            pltpu.VMEM((4, 4, 2, MSG_B, 128), BF),
            pltpu.VMEM((4, 4, 2, MSG_B, 128), BF),
            pltpu.VMEM((2, 4, 4, MSG_B, 128), BF),
            pltpu.VMEM((CELLS, 128, CH), BF),
            pltpu.VMEM((CELLS, 64, CH), BF),
            pltpu.VMEM((4, CELLS, 64, CH), BF),
            pltpu.VMEM((64, 128), F32),
            dma((11,)), dma((7,)), dma((4,)), dma((4,)), dma((4,)), dma((4,)), dma((4,)), dma((4,)),
            dma, dma,
        ],
        compiler_params=pltpu.CompilerParams(
            collective_id=0, has_side_effects=True, vmem_limit_bytes=LIM
        ),
        name="front",
    )(latent, owner, nexts, cache_latent, cache_act, weight_in, bias_in, gain, shift, sel, rest)


def decode_kernel(
    trans_hbm, feat_hbm, live_hbm, later_hbm, w_in_hbm, bias_hbm, gain_hbm, shift_hbm,
    bias_mid_hbm, sel_hbm, rest_hbm, w_mid_hbm,
    feat_out_hbm, conv_hbm, nlat_hbm, nact_hbm,
    trans, feat, live_v, later_v, w_in, bias_v, gain_v, shift_v, bias_mid_v, sel, rest, w_mid,
    sums, mixed, wide_out, nact_out, nlat_out,
    sem_in, sem_w, sem_out,
):
    loads = [
        pltpu.make_async_copy(src, dst, sem_in.at[i])
        for i, (src, dst) in enumerate((
            (later_hbm, later_v), (sel_hbm, sel), (rest_hbm, rest), (w_in_hbm, w_in),
            (bias_hbm, bias_v), (gain_hbm, gain_v), (shift_hbm, shift_v),
            (bias_mid_hbm, bias_mid_v), (live_hbm, live_v), (feat_hbm, feat),
            (trans_hbm, trans),
        ))
    ]
    for load in loads:
        load.start()
    w_copies = [
        pltpu.make_async_copy(
            w_mid_hbm.at[:, pl.ds(tap * CH, CH), :], w_mid.at[at % (AHEAD + 1)], sem_w.at[at]
        )
        for at, tap in enumerate(TAPS)
    ]
    for copy in w_copies[:AHEAD]:
        copy.start()

    groups = block_ones()
    for load in loads[:9]:
        load.wait()
    got = later_v[...].reshape(N_DEC * MSG_B, 128)
    w_cat = input_weights(w_in)
    bias = bias_v[...].reshape(1, CH)
    gain = gain_v[...].reshape(1, CH)
    shift = shift_v[...].reshape(1, CH)
    bias_mid = bias_mid_v[...].reshape(1, CH)
    flags = lax.dot_general(
        onehot(iota((8, 128), 1) == 0), got, (((1,), (1,)), ((), ())),
        preferred_element_type=F32,
    )
    flags = onehot(flags < 100.0)

    def entry_of(row):
        core, zz, xx, k = row // 256, (row // 64) % 4, (row // 16) % 4, (row // PART) % 2
        return (xx * 8 + zz * 2 + core) * CAP_C + k

    big = iota((512, 128), 0)
    held = dot(flags, onehot((big % PART == 0) & (entry_of(big) == iota((512, 128), 1))))
    before = onehot(iota((128, 128), 0) < iota((128, 128), 1))
    place = dot(held.astype(BF), before)
    take = onehot((held[:1] > 0.5) & (place[:1] == iota((32, 128), 0).astype(F32)))
    lane = iota((128, 512), 1)
    entry = entry_of(lane) == iota((128, 512), 0)
    take = dot(take, onehot(entry)).astype(BF)
    wide = jnp.concatenate([take] * 4, axis=0)
    kind = iota((128, 512), 0) // 32
    halves = [
        dot(jnp.where(iota((128, 512), 1) % PART == kind * 2 + half, wide, 0), got)
        for half in range(2)
    ]
    moved = jnp.concatenate(halves, axis=1)
    live_next = jnp.where(moved[:64, :1] < 32.0, 1.0, 0.0)
    fresh = jnp.where(moved > 32.0, 0.0, moved).astype(BF)
    pair = onehot(iota((64, 64), 1) == (iota((64, 64), 0) % 2) * 32 + iota((64, 64), 0) // 2)
    nlat_out[...] = dot(pair, fresh[64:]).astype(BF).reshape(32, 2, 256)
    outs = [pltpu.make_async_copy(nlat_out, nlat_hbm, sem_out.at[0])]
    outs[0].start()

    def put_mixed(cell, value):
        mixed[cell] = value

    features_of(patches(fresh, 64, sel, rest), 64, w_cat, bias, live_next, put_mixed,
                (REST_CELLS, PLAIN_CELLS))

    def put_next(cell, value):
        value = (value.astype(F32) * live_next).astype(BF)
        nact_out[:, :, cell * CH:(cell + 1) * CH] = dot(pair, value).astype(BF).reshape(32, 2, CH)

    normalised(lambda cell: mixed[cell], put_next, 64, groups, gain, shift)
    out = pltpu.make_async_copy(nact_out, nact_hbm, sem_out.at[1])
    out.start()
    outs.append(out)

    loads[9].wait()
    order = onehot(
        iota((128, 128), 1) == (iota((128, 128), 0) % 4) * 32 + iota((128, 128), 0) // 4
    )
    for cell in range(CELLS):
        turned = dot(order, feat[cell]).astype(BF).reshape(32, 4, CH)
        wide_out[:, :, cell * CH:(cell + 1) * CH] = turned
    feat_copy = pltpu.make_async_copy(wide_out, feat_out_hbm, sem_out.at[2])
    feat_copy.start()

    loads[10].wait()
    for at, tap in enumerate(TAPS):
        if at + AHEAD < len(TAPS):
            w_copies[at + AHEAD].start()
        w_copies[at].wait()
        here = at % (AHEAD + 1)
        g0 = w_mid[here, 0].astype(F32)
        g1 = w_mid[here, 1].astype(F32)
        g2 = w_mid[here, 2].astype(F32)
        ends = g0 + g2
        weights = [
            w_mid[here, 0], ((ends + g1) * 0.5).astype(BF), ((ends - g1) * 0.5).astype(BF),
            w_mid[here, 2],
        ]
        pairs = tap_cells(tap)
        for j in range(4):
            left = jnp.concatenate([trans[j, source] for _, source in pairs], axis=0)
            made = dot(left, weights[j])
            for i, (cell, _) in enumerate(pairs):
                piece = made[i * 64:(i + 1) * 64]
                if at == 0:
                    sums[j, cell] = piece
                else:
                    sums[j, cell] += piece

    r128 = iota((128, 128), 0)
    back = onehot(iota((128, 128), 1) == (r128 % 2) * 64 + ((r128 % 4) // 2) * 32 + r128 // 4)
    keep = live_v[...][:, :1]
    feat_copy.wait()
    for cell in range(CELLS):
        both = sums[1, cell] + sums[2, cell]
        apart = sums[1, cell] - sums[2, cell]
        even = ((sums[0, cell] + both + bias_mid) * keep).astype(BF)
        odd = ((apart - sums[3, cell] + bias_mid) * keep).astype(BF)
        turned = dot(back, jnp.concatenate([even, odd], axis=0)).astype(BF)
        wide_out[:, :, cell * CH:(cell + 1) * CH] = turned.reshape(32, 4, CH)
        if cell % 4 == 3:
            lanes = pl.ds((cell - 3) * CH, 4 * CH)
            out = pltpu.make_async_copy(
                wide_out.at[:, :, lanes], conv_hbm.at[:, :, lanes], sem_out.at[3 + cell // 4]
            )
            out.start()
            outs.append(out)
    for out in outs:
        out.wait()


def decode(trans, feat, live, later, weight_in, bias_in, gain, shift, bias_mid, sel, rest,
           weight_mid):
    hbm = pl.BlockSpec(memory_space=pltpu.HBM)
    wide = CELLS * CH
    dma = pltpu.SemaphoreType.DMA
    return pl.pallas_call(
        decode_kernel,
        out_shape=(
            jax.ShapeDtypeStruct((DSLOTS, FR, wide), BF),
            jax.ShapeDtypeStruct((DSLOTS, FR, wide), BF),
            jax.ShapeDtypeStruct((DSLOTS, 2, LAT * CELLS), BF),
            jax.ShapeDtypeStruct((DSLOTS, 2, wide), BF),
        ),
        in_specs=[hbm] * 12,
        out_specs=(hbm,) * 4,
        scratch_shapes=[
            pltpu.VMEM((4, CELLS, 64, CH), BF),
            pltpu.VMEM((CELLS, 128, CH), BF),
            pltpu.VMEM((64, 128), F32),
            pltpu.VMEM((2, 4, 4, MSG_B, 128), BF),
            pltpu.VMEM((3, 9 * LAT, CH), BF),
            pltpu.VMEM((CH,), F32),
            pltpu.VMEM((CH,), F32),
            pltpu.VMEM((CH,), F32),
            pltpu.VMEM((CH,), F32),
            pltpu.VMEM(sel.shape, BF),
            pltpu.VMEM(rest.shape, BF),
            pltpu.VMEM((AHEAD + 1, 3, CH, CH), BF),
            pltpu.VMEM((4, CELLS, 64, CH), F32),
            pltpu.VMEM((CELLS, 64, CH), BF),
            pltpu.VMEM((DSLOTS, FR, wide), BF),
            pltpu.VMEM((DSLOTS, 2, wide), BF),
            pltpu.VMEM((DSLOTS, 2, LAT * CELLS), BF),
            dma((11,)), dma((9,)), dma((7,)),
        ],
        compiler_params=pltpu.CompilerParams(vmem_limit_bytes=LIM),
        name="decode",
    )(trans, feat, live, later, weight_in, bias_in, gain, shift, bias_mid, sel, rest, weight_mid)


def shards(latent, latent_owner, next_owner, cache_latent, cache_act, weight_in, bias_in,
           norm_gain, norm_shift, weight_mid, bias_mid):
    sel, rest = patch_selectors()
    made = front(
        latent, latent_owner.reshape(1, GEN), next_owner.reshape(1, DSLOTS), cache_latent,
        cache_act, weight_in, bias_in, norm_gain, norm_shift, sel, rest,
    )
    return decode(*made, weight_in, bias_in, norm_gain, norm_shift, bias_mid, sel, rest, weight_mid)


def solution(mesh):
    both = ("gen", "dec")
    in_specs = (
        P(both, None, None), P(both, None), P(both), P(both, None, None), P(both, None, None),
        P(), P(), P(), P(), P(), P(),
    )
    out_specs = (P(both, None, None),) * 4
    return jax.shard_map(shards, mesh=mesh, in_specs=in_specs, out_specs=out_specs, check_vma=False)
```

```python
import functools

import jax
import jax.numpy as jnp
import numpy as np
from jax import lax
from jax.experimental import pallas as pl
from jax.experimental.pallas import tpu as pltpu
from jax.sharding import PartitionSpec as P

BF = jnp.bfloat16
F32 = jnp.float32
I32 = jnp.int32

N_GEN, N_DEC = 4, 32
GEN, CAP_L, DSLOTS, CAP_C = 24, 8, 32, 2
FR, CELLS, HT, WT, LAT, CH = 4, 16, 4, 4, 16, 512
PART = 8
MSG_A = CAP_L * PART
MSG_B = CAP_C * PART
DEAD, EMPTY = 64.0, 128.0
EPSILON = 1e-06

AHEAD = 3
LIM = 65400 << 10
TAPS = [4, 1, 3, 5, 7, 0, 2, 6, 8]
REST_CELLS = [y * WT + x for y in range(3) for x in range(3)]
PLAIN_CELLS = [c for c in range(CELLS) if c not in REST_CELLS]


def tap_cells(tap):
    dy, dx = tap // 3 - 1, tap % 3 - 1
    pairs = []
    for y in range(HT):
        for x in range(WT):
            if 0 <= y + dy < HT and 0 <= x + dx < WT:
                pairs.append((y * WT + x, (y + dy) * WT + x + dx))
    return pairs


def patch_selectors():
    first = np.zeros((LAT * CELLS, CELLS * 128), np.float32)
    for tap in range(8):
        for cell, source in tap_cells(tap):
            for e in range(LAT):
                first[e * CELLS + source, cell * 128 + tap * LAT + e] = 1
    rest = np.zeros((3 * LAT * CELLS, len(REST_CELLS) * 128), np.float32)
    for cell, source in tap_cells(8):
        at = REST_CELLS.index(cell)
        for a in range(3):
            for e in range(LAT):
                rest[a * 256 + e * CELLS + source, at * 128 + a * LAT + e] = 1
    return jnp.asarray(first, BF), jnp.asarray(rest, BF)


def dot(a, b):
    return jnp.dot(a, b, preferred_element_type=F32)


def iota(shape, dim):
    return lax.broadcasted_iota(I32, shape, dim)


def onehot(mask):
    return jnp.where(mask, 1.0, 0.0).astype(BF)


def ranked_codes(row, length, per):
    sub = iota((length, length), 0)
    lane = iota((length, length), 1)
    wide = jnp.broadcast_to(row, (length, length))
    col = jnp.sum(jnp.where(sub == lane, wide, 0.0), axis=1, keepdims=True)
    same = (wide == col) & (lane < sub)
    rank = jnp.sum(jnp.where(same, 1.0, 0.0), axis=1, keepdims=True)
    return col * per + rank


def spread(codes, where_to, length, width):
    hit = iota((length, width), 0) == where_to
    found = jnp.sum(jnp.where(hit, codes + 1.0, 0.0), axis=0, keepdims=True)
    return found - 1.0


def group_mean(total, spread_groups):
    high = total.astype(BF)
    left = total - high.astype(F32)
    mid = left.astype(BF)
    low = (left - mid.astype(F32)).astype(BF)
    return dot(high, spread_groups) + dot(mid, spread_groups) + dot(low, spread_groups)


def silu(u):
    half = 0.5 * u
    return half + half * jnp.tanh(half)


def block_ones():
    same = (iota((CH, CH), 0) // 16) == (iota((CH, CH), 1) // 16)
    return jnp.where(same, 1.0 / 256.0, 0.0).astype(BF)


def input_weights(w_in_ref):
    return jnp.concatenate(
        [w_in_ref[a, :128, :] for a in range(3)]
        + [w_in_ref[a, 128:144, :] for a in range(3)]
        + [jnp.zeros((80, CH), BF)],
        axis=0,
    )


def normalised(read, write, rows, groups, gain, shift):
    total = jnp.zeros((rows, CH), F32)
    for c in range(CELLS):
        total = total + read(c).astype(F32)
    center = group_mean(total, groups)
    square = jnp.zeros((rows, CH), F32)
    for c in range(CELLS):
        off = read(c).astype(F32) - center
        square = square + off * off
    scale = lax.rsqrt(group_mean(square, groups) + EPSILON) * gain
    for c in range(CELLS):
        u = (read(c).astype(F32) - center) * scale + shift
        write(c, silu(u).astype(BF))


def patches(frames, rows, sel, rest):
    shifted = [frames[a * 32:a * 32 + rows] for a in range(3)]
    return (
        dot(frames, sel[...]).astype(BF),
        dot(jnp.concatenate(shifted, axis=1), rest[...]).astype(BF),
    )


def features_of(found, rows, w_cat, bias, live, write, groups):
    taps, rest = found
    for cells in groups:
        depth = 512 if cells[0] in REST_CELLS else 384
        left = []
        for c in cells:
            block = [taps[a * 32:a * 32 + rows, c * 128:c * 128 + 128] for a in range(3)]
            if depth == 512:
                at = REST_CELLS.index(c)
                block.append(rest[:, at * 128:at * 128 + 128])
            left.append(jnp.concatenate(block, axis=1))
        made = dot(jnp.concatenate(left, axis=0), w_cat[:depth])
        for i, c in enumerate(cells):
            write(c, ((made[i * rows:(i + 1) * rows] + bias) * live).astype(BF))


def lane_halves(pick_row, pick_col_of, source):
    return jnp.concatenate(
        [dot(onehot(pick_row == pick_col_of(half)), source) for half in range(2)], axis=1
    )


def front_kernel(
    latent_hbm, owner_hbm, next_hbm, cache_hbm, hist_hbm, w_in_hbm, bias_hbm, gain_hbm,
    shift_hbm, sel_hbm, rest_hbm,
    trans_hbm, feat_hbm, live_hbm, later_hbm,
    latent, owner, nexts, cache, hist, w_in, bias_v, gain_v, shift_v, sel, rest,
    send_a, recv_a, send_b, recv_x, recv_e, feat, old, trans, live_v,
    sem_in, sem_out, sem_sa, sem_ra, sem_sx, sem_rx, sem_se, sem_re,
):
    g = lax.axis_index("gen")
    d = lax.axis_index("dec")
    x, e = d // 8, d % 8
    gens = [lax.rem(g + i, 4) for i in (1, 2, 3)]
    xs = [lax.rem(x + i, 4) for i in (1, 2, 3)]
    es = [lax.rem(e + i, 8) for i in range(1, 8)]
    mesh_ids = pl.DeviceIdType.MESH
    barrier = pltpu.get_barrier_semaphore()
    peers = [{"gen": p} for p in gens]
    peers += [{"dec": p * 8 + e} for p in xs]
    peers += [{"dec": x * 8 + p} for p in es]
    for peer in peers:
        pl.semaphore_signal(barrier, inc=1, device_id=peer, device_id_type=mesh_ids)

    loads = []
    for i, (src, dst) in enumerate((
        (latent_hbm, latent), (owner_hbm, owner), (next_hbm, nexts), (cache_hbm, cache),
        (hist_hbm, hist), (sel_hbm, sel), (rest_hbm, rest), (w_in_hbm, w_in),
        (bias_hbm, bias_v), (gain_hbm, gain_v), (shift_hbm, shift_v),
    )):
        load = pltpu.make_async_copy(src, dst, sem_in.at[i])
        load.start()
        loads.append(load)

    loads[0].wait()
    loads[1].wait()
    loads[2].wait()
    codes = ranked_codes(owner[...].astype(F32), GEN, CAP_L)
    lane = iota((GEN, 256), 1)
    clip_at = jnp.where(lane < 192, (lane % 96) // 4, -1)
    lanes = spread(codes, clip_at, GEN, 256)
    row = iota((N_GEN * MSG_A, 256), 0)
    col = iota((N_GEN * MSG_A, 256), 1)
    named = ((row // MSG_A) * CAP_L + (row % MSG_A) // PART).astype(F32) == lanes
    pick = named & ((row % PART) == (col % 4) * 2 + col // 96) & (col < 192)
    present = jnp.sum(jnp.where(pick, 1.0, 0.0), axis=1, keepdims=True)
    rows = latent[...].reshape(GEN * FR, LAT * CELLS)
    rows = jnp.concatenate([rows[:, :128], rows[:, 128:], jnp.zeros((64, 128), BF)], axis=0)
    ready = jnp.where(present > 0.5, dot(onehot(pick), rows), DEAD)
    send_a[...] = ready.astype(BF).reshape(send_a.shape)
    recv_a[g] = send_a[g]

    pl.semaphore_wait(barrier, len(peers))

    def copy_a(target, landed):
        return pltpu.make_async_remote_copy(
            src_ref=send_a.at[target], dst_ref=recv_a.at[landed],
            send_sem=sem_sa.at[target], recv_sem=sem_ra.at[landed],
            device_id={"gen": target}, device_id_type=mesh_ids,
        )

    for p in gens:
        copy_a(p, g).start()

    codes_b = ranked_codes(nexts[...].astype(F32), DSLOTS, CAP_C)
    lane_b = iota((DSLOTS, 256), 1)
    lanes_b = spread(codes_b, lane_b // PART, DSLOTS, 256)
    row_b = iota((N_DEC * MSG_B, 256), 0)
    col_b = iota((N_DEC * MSG_B, 256), 1)
    pick_b = ((row_b // PART).astype(F32) == lanes_b) & ((row_b % PART) == (col_b % PART))
    filled = jnp.sum(jnp.where(pick_b, 1.0, 0.0), axis=1, keepdims=True)
    pick_b = onehot(pick_b)
    loads[4].wait()
    turn = onehot(iota((64, 64), 1) == (iota((64, 64), 0) % 32) * 2 + iota((64, 64), 0) // 32)
    for cell in range(CELLS):
        lanes_c = slice(cell * CH, (cell + 1) * CH)
        old[cell] = dot(turn, hist[:, :, lanes_c].reshape(64, CH)).astype(BF)
    loads[3].wait()
    for load in loads[5:]:
        load.wait()
    groups = block_ones()
    w_cat = input_weights(w_in)
    bias = bias_v[...].reshape(1, CH)
    gain = gain_v[...].reshape(1, CH)
    shift = shift_v[...].reshape(1, CH)
    cached = dot(turn, cache[...].reshape(64, 256)).astype(BF)

    for p in gens:
        copy_a(p, p).wait_recv()
    got = recv_a[...].reshape(N_GEN * MSG_A, 128)
    messages = jnp.where(filled > 0.5, dot(pick_b, got), EMPTY)
    send_b[...] = messages.astype(BF).reshape(send_b.shape)

    def copy_x(target, landed):
        return pltpu.make_async_remote_copy(
            src_ref=send_b.at[target], dst_ref=recv_x.at[landed],
            send_sem=sem_sx.at[target], recv_sem=sem_rx.at[landed],
            device_id={"dec": target * 8 + e}, device_id_type=mesh_ids,
        )

    def copy_e(target, landed):
        return pltpu.make_async_remote_copy(
            src_ref=recv_x.at[:, target], dst_ref=recv_e.at[landed],
            send_sem=sem_se.at[target], recv_sem=sem_re.at[landed],
            device_id={"dec": x * 8 + target}, device_id_type=mesh_ids,
        )

    for p in xs:
        copy_x(p, x).start()
    recv_x[x] = send_b[x]

    r128 = iota((128, 256), 0)
    placed = lane_halves(
        iota((128, 256), 1), lambda half: (r128 % 32) * PART + (r128 // 32) * 2 + half, got
    )
    live = jnp.where(placed[:, :1] < 32.0, 1.0, 0.0)
    live_v[...] = jnp.broadcast_to(live[:64], (64, 128))
    fresh = jnp.where(placed > 32.0, 0.0, placed).astype(BF)
    found = patches(jnp.concatenate([cached, fresh], axis=0), 128, sel, rest)

    def put_feat(cell, value):
        feat[cell] = value

    features_of(found, 128, w_cat, bias, live, put_feat, (REST_CELLS,))

    for p in xs:
        copy_x(p, p).wait_recv()
    for p in es:
        copy_e(p, e).start()
    recv_e[e] = recv_x[:, e]

    features_of(found, 128, w_cat, bias, live, put_feat, (PLAIN_CELLS,))
    outs = [pltpu.make_async_copy(feat, feat_hbm, sem_out.at[0]),
            pltpu.make_async_copy(live_v, live_hbm, sem_out.at[1])]
    for out in outs:
        out.start()

    total = jnp.zeros((128, CH), F32)
    for cell in range(CELLS):
        total = total + feat[cell].astype(F32)
    center = group_mean(total, groups)
    square = jnp.zeros((128, CH), F32)
    for cell in range(CELLS):
        off = feat[cell].astype(F32) - center
        square = square + off * off
    scale = lax.rsqrt(group_mean(square, groups) + EPSILON) * gain

    for cell in range(CELLS):
        u = (feat[cell].astype(F32) - center) * scale + shift
        act = silu(u).astype(BF)
        q = [old[cell, :32], old[cell, 32:]] + [act[t * 32:t * 32 + 32] for t in range(4)]
        for tile in range(2):
            d0, d1, d2, d3 = q[2 * tile:2 * tile + 4]
            at = slice(tile * 32, tile * 32 + 32)
            trans[0, cell, at] = d0 - d2
            trans[1, cell, at] = d1 + d2
            trans[2, cell, at] = d2 - d1
            trans[3, cell, at] = d1 - d3
        if cell % 4 == 3:
            part = pl.ds(cell - 3, 4)
            out = pltpu.make_async_copy(
                trans.at[:, part], trans_hbm.at[:, part], sem_out.at[2 + cell // 4]
            )
            out.start()
            outs.append(out)

    for p in es:
        copy_e(p, p).wait_recv()
    out = pltpu.make_async_copy(recv_e, later_hbm, sem_out.at[6])
    out.start()
    outs.append(out)
    for p in gens:
        copy_a(p, g).wait_send()
    for p in xs:
        copy_x(p, x).wait_send()
    for p in es:
        copy_e(p, e).wait_send()
    for out in outs:
        out.wait()


def front(latent, owner, nexts, cache_latent, cache_act, weight_in, bias_in, gain, shift, sel, rest):
    hbm = pl.BlockSpec(memory_space=pltpu.HBM)
    wide = CELLS * CH
    dma = pltpu.SemaphoreType.DMA
    return pl.pallas_call(
        front_kernel,
        out_shape=(
            jax.ShapeDtypeStruct((4, CELLS, 64, CH), BF),
            jax.ShapeDtypeStruct((CELLS, 128, CH), BF),
            jax.ShapeDtypeStruct((64, 128), F32),
            jax.ShapeDtypeStruct((8, 4, MSG_B, 128), BF),
        ),
        in_specs=[hbm] * 11,
        out_specs=(hbm,) * 4,
        scratch_shapes=[
            pltpu.VMEM((GEN, FR, LAT * CELLS), BF),
            pltpu.VMEM((1, GEN), I32),
            pltpu.VMEM((1, DSLOTS), I32),
            pltpu.VMEM((DSLOTS, 2, LAT * CELLS), BF),
            pltpu.VMEM((DSLOTS, 2, wide), BF),
            pltpu.VMEM((3, 9 * LAT, CH), BF),
            pltpu.VMEM((CH,), F32),
            pltpu.VMEM((CH,), F32),
            pltpu.VMEM((CH,), F32),
            pltpu.VMEM(sel.shape, BF),
            pltpu.VMEM(rest.shape, BF),
            pltpu.VMEM((N_GEN, MSG_A, 128), BF),
            pltpu.VMEM((N_GEN, MSG_A, 128), BF),
            pltpu.VMEM((4, 8, MSG_B, 128), BF),
            pltpu.VMEM((4, 8, MSG_B, 128), BF),
            pltpu.VMEM((8, 4, MSG_B, 128), BF),
            pltpu.VMEM((CELLS, 128, CH), BF),
            pltpu.VMEM((CELLS, 64, CH), BF),
            pltpu.VMEM((4, CELLS, 64, CH), BF),
            pltpu.VMEM((64, 128), F32),
            dma((11,)), dma((7,)), dma((4,)), dma((4,)), dma((4,)), dma((4,)), dma((8,)), dma((8,)),
        ],
        compiler_params=pltpu.CompilerParams(
            collective_id=0, has_side_effects=True, vmem_limit_bytes=LIM
        ),
        name="front",
    )(latent, owner, nexts, cache_latent, cache_act, weight_in, bias_in, gain, shift, sel, rest)


def decode_kernel(
    trans_hbm, feat_hbm, live_hbm, later_hbm, w_in_hbm, bias_hbm, gain_hbm, shift_hbm,
    bias_mid_hbm, sel_hbm, rest_hbm, w_mid_hbm,
    feat_out_hbm, conv_hbm, nlat_hbm, nact_hbm,
    trans, feat, live_v, later_v, w_in, bias_v, gain_v, shift_v, bias_mid_v, sel, rest, w_mid,
    sums, mixed, wide_out, nact_out, nlat_out,
    sem_in, sem_w, sem_out,
):
    loads = [
        pltpu.make_async_copy(src, dst, sem_in.at[i])
        for i, (src, dst) in enumerate((
            (later_hbm, later_v), (sel_hbm, sel), (rest_hbm, rest), (w_in_hbm, w_in),
            (bias_hbm, bias_v), (gain_hbm, gain_v), (shift_hbm, shift_v),
            (bias_mid_hbm, bias_mid_v), (live_hbm, live_v), (feat_hbm, feat),
            (trans_hbm, trans),
        ))
    ]
    for load in loads:
        load.start()
    w_copies = [
        pltpu.make_async_copy(
            w_mid_hbm.at[:, pl.ds(tap * CH, CH), :], w_mid.at[at % (AHEAD + 1)], sem_w.at[at]
        )
        for at, tap in enumerate(TAPS)
    ]
    for copy in w_copies[:AHEAD]:
        copy.start()

    groups = block_ones()
    for load in loads[:9]:
        load.wait()
    got = later_v[...].reshape(N_DEC * MSG_B, 128)
    w_cat = input_weights(w_in)
    bias = bias_v[...].reshape(1, CH)
    gain = gain_v[...].reshape(1, CH)
    shift = shift_v[...].reshape(1, CH)
    bias_mid = bias_mid_v[...].reshape(1, CH)
    flags = lax.dot_general(
        onehot(iota((8, 128), 1) == 0), got, (((1,), (1,)), ((), ())),
        preferred_element_type=F32,
    )
    flags = onehot(flags < 100.0)

    def entry_of(row):
        return (((row // 16) % 4) * 8 + row // 64) * CAP_C + (row // PART) % CAP_C

    big = iota((512, 128), 0)
    held = dot(flags, onehot((big % PART == 0) & (entry_of(big) == iota((512, 128), 1))))
    before = onehot(iota((128, 128), 0) < iota((128, 128), 1))
    place = dot(held.astype(BF), before)
    take = onehot((held[:1] > 0.5) & (place[:1] == iota((32, 128), 0).astype(F32)))
    lane = iota((128, 512), 1)
    entry = entry_of(lane) == iota((128, 512), 0)
    take = dot(take, onehot(entry)).astype(BF)
    wide = jnp.concatenate([take] * 4, axis=0)
    kind = iota((128, 512), 0) // 32
    halves = [
        dot(jnp.where(iota((128, 512), 1) % PART == kind * 2 + half, wide, 0), got)
        for half in range(2)
    ]
    moved = jnp.concatenate(halves, axis=1)
    live_next = jnp.where(moved[:64, :1] < 32.0, 1.0, 0.0)
    fresh = jnp.where(moved > 32.0, 0.0, moved).astype(BF)
    pair = onehot(iota((64, 64), 1) == (iota((64, 64), 0) % 2) * 32 + iota((64, 64), 0) // 2)
    nlat_out[...] = dot(pair, fresh[64:]).astype(BF).reshape(32, 2, 256)
    outs = [pltpu.make_async_copy(nlat_out, nlat_hbm, sem_out.at[0])]
    outs[0].start()

    def put_mixed(cell, value):
        mixed[cell] = value

    features_of(patches(fresh, 64, sel, rest), 64, w_cat, bias, live_next, put_mixed,
                (REST_CELLS, PLAIN_CELLS))

    def put_next(cell, value):
        value = (value.astype(F32) * live_next).astype(BF)
        nact_out[:, :, cell * CH:(cell + 1) * CH] = dot(pair, value).astype(BF).reshape(32, 2, CH)

    normalised(lambda cell: mixed[cell], put_next, 64, groups, gain, shift)
    out = pltpu.make_async_copy(nact_out, nact_hbm, sem_out.at[1])
    out.start()
    outs.append(out)

    loads[9].wait()
    order = onehot(
        iota((128, 128), 1) == (iota((128, 128), 0) % 4) * 32 + iota((128, 128), 0) // 4
    )
    for cell in range(CELLS):
        turned = dot(order, feat[cell]).astype(BF).reshape(32, 4, CH)
        wide_out[:, :, cell * CH:(cell + 1) * CH] = turned
    feat_copy = pltpu.make_async_copy(wide_out, feat_out_hbm, sem_out.at[2])
    feat_copy.start()

    loads[10].wait()
    for at, tap in enumerate(TAPS):
        if at + AHEAD < len(TAPS):
            w_copies[at + AHEAD].start()
        w_copies[at].wait()
        here = at % (AHEAD + 1)
        g0 = w_mid[here, 0].astype(F32)
        g1 = w_mid[here, 1].astype(F32)
        g2 = w_mid[here, 2].astype(F32)
        ends = g0 + g2
        weights = [
            w_mid[here, 0], ((ends + g1) * 0.5).astype(BF), ((ends - g1) * 0.5).astype(BF),
            w_mid[here, 2],
        ]
        pairs = tap_cells(tap)
        for j in range(4):
            left = jnp.concatenate([trans[j, source] for _, source in pairs], axis=0)
            made = dot(left, weights[j])
            for i, (cell, _) in enumerate(pairs):
                piece = made[i * 64:(i + 1) * 64]
                if at == 0:
                    sums[j, cell] = piece
                else:
                    sums[j, cell] += piece

    r128 = iota((128, 128), 0)
    back = onehot(iota((128, 128), 1) == (r128 % 2) * 64 + ((r128 % 4) // 2) * 32 + r128 // 4)
    keep = live_v[...][:, :1]
    feat_copy.wait()
    for cell in range(CELLS):
        both = sums[1, cell] + sums[2, cell]
        apart = sums[1, cell] - sums[2, cell]
        even = ((sums[0, cell] + both + bias_mid) * keep).astype(BF)
        odd = ((apart - sums[3, cell] + bias_mid) * keep).astype(BF)
        turned = dot(back, jnp.concatenate([even, odd], axis=0)).astype(BF)
        wide_out[:, :, cell * CH:(cell + 1) * CH] = turned.reshape(32, 4, CH)
        if cell % 4 == 3:
            lanes = pl.ds((cell - 3) * CH, 4 * CH)
            out = pltpu.make_async_copy(
                wide_out.at[:, :, lanes], conv_hbm.at[:, :, lanes], sem_out.at[3 + cell // 4]
            )
            out.start()
            outs.append(out)
    for out in outs:
        out.wait()


def decode(trans, feat, live, later, weight_in, bias_in, gain, shift, bias_mid, sel, rest,
           weight_mid):
    hbm = pl.BlockSpec(memory_space=pltpu.HBM)
    wide = CELLS * CH
    dma = pltpu.SemaphoreType.DMA
    return pl.pallas_call(
        decode_kernel,
        out_shape=(
            jax.ShapeDtypeStruct((DSLOTS, FR, wide), BF),
            jax.ShapeDtypeStruct((DSLOTS, FR, wide), BF),
            jax.ShapeDtypeStruct((DSLOTS, 2, LAT * CELLS), BF),
            jax.ShapeDtypeStruct((DSLOTS, 2, wide), BF),
        ),
        in_specs=[hbm] * 12,
        out_specs=(hbm,) * 4,
        scratch_shapes=[
            pltpu.VMEM((4, CELLS, 64, CH), BF),
            pltpu.VMEM((CELLS, 128, CH), BF),
            pltpu.VMEM((64, 128), F32),
            pltpu.VMEM((8, 4, MSG_B, 128), BF),
            pltpu.VMEM((3, 9 * LAT, CH), BF),
            pltpu.VMEM((CH,), F32),
            pltpu.VMEM((CH,), F32),
            pltpu.VMEM((CH,), F32),
            pltpu.VMEM((CH,), F32),
            pltpu.VMEM(sel.shape, BF),
            pltpu.VMEM(rest.shape, BF),
            pltpu.VMEM((AHEAD + 1, 3, CH, CH), BF),
            pltpu.VMEM((4, CELLS, 64, CH), F32),
            pltpu.VMEM((CELLS, 64, CH), BF),
            pltpu.VMEM((DSLOTS, FR, wide), BF),
            pltpu.VMEM((DSLOTS, 2, wide), BF),
            pltpu.VMEM((DSLOTS, 2, LAT * CELLS), BF),
            dma((11,)), dma((9,)), dma((7,)),
        ],
        compiler_params=pltpu.CompilerParams(vmem_limit_bytes=LIM),
        name="decode",
    )(trans, feat, live, later, weight_in, bias_in, gain, shift, bias_mid, sel, rest, weight_mid)


def shards(latent, latent_owner, next_owner, cache_latent, cache_act, weight_in, bias_in,
           norm_gain, norm_shift, weight_mid, bias_mid):
    sel, rest = patch_selectors()
    made = front(
        latent, latent_owner.reshape(1, GEN), next_owner.reshape(1, DSLOTS), cache_latent,
        cache_act, weight_in, bias_in, norm_gain, norm_shift, sel, rest,
    )
    return decode(*made, weight_in, bias_in, norm_gain, norm_shift, bias_mid, sel, rest, weight_mid)


def solution(mesh):
    both = ("gen", "dec")
    in_specs = (
        P(both, None, None), P(both, None), P(both), P(both, None, None), P(both, None, None),
        P(), P(), P(), P(), P(), P(),
    )
    out_specs = (P(both, None, None),) * 4
    return jax.shard_map(shards, mesh=mesh, in_specs=in_specs, out_specs=out_specs, check_vma=False)
```

```python
import functools

import jax
import jax.numpy as jnp
import numpy as np
from jax import lax
from jax.experimental import pallas as pl
from jax.experimental.pallas import tpu as pltpu
from jax.sharding import PartitionSpec as P

BF = jnp.bfloat16
F32 = jnp.float32
I32 = jnp.int32

N_GEN, N_DEC = 4, 32
GEN, CAP_L, DSLOTS, CAP_C = 24, 8, 32, 2
FR, CELLS, HT, WT, LAT, CH = 4, 16, 4, 4, 16, 512
PART = 8
MSG_A = CAP_L * PART
MSG_B = CAP_C * PART
DEAD, EMPTY = 64.0, 128.0
EPSILON = 1e-06

AHEAD = 3
LIM = 65400 << 10
TAPS = [4, 1, 3, 5, 7, 0, 2, 6, 8]
REST_CELLS = [y * WT + x for y in range(3) for x in range(3)]
PLAIN_CELLS = [c for c in range(CELLS) if c not in REST_CELLS]


def tap_cells(tap):
    dy, dx = tap // 3 - 1, tap % 3 - 1
    pairs = []
    for y in range(HT):
        for x in range(WT):
            if 0 <= y + dy < HT and 0 <= x + dx < WT:
                pairs.append((y * WT + x, (y + dy) * WT + x + dx))
    return pairs


def patch_selectors():
    first = np.zeros((LAT * CELLS, CELLS * 128), np.float32)
    for tap in range(8):
        for cell, source in tap_cells(tap):
            for e in range(LAT):
                first[e * CELLS + source, cell * 128 + tap * LAT + e] = 1
    rest = np.zeros((3 * LAT * CELLS, len(REST_CELLS) * 128), np.float32)
    for cell, source in tap_cells(8):
        at = REST_CELLS.index(cell)
        for a in range(3):
            for e in range(LAT):
                rest[a * 256 + e * CELLS + source, at * 128 + a * LAT + e] = 1
    return jnp.asarray(first, BF), jnp.asarray(rest, BF)


def dot(a, b):
    return jnp.dot(a, b, preferred_element_type=F32)


def iota(shape, dim):
    return lax.broadcasted_iota(I32, shape, dim)


def onehot(mask):
    return jnp.where(mask, 1.0, 0.0).astype(BF)


def ranked_codes(row, length, per):
    sub = iota((length, length), 0)
    lane = iota((length, length), 1)
    wide = jnp.broadcast_to(row, (length, length))
    col = jnp.sum(jnp.where(sub == lane, wide, 0.0), axis=1, keepdims=True)
    same = (wide == col) & (lane < sub)
    rank = jnp.sum(jnp.where(same, 1.0, 0.0), axis=1, keepdims=True)
    return col * per + rank


def spread(codes, where_to, length, width):
    hit = iota((length, width), 0) == where_to
    found = jnp.sum(jnp.where(hit, codes + 1.0, 0.0), axis=0, keepdims=True)
    return found - 1.0


def group_mean(total, spread_groups):
    high = total.astype(BF)
    left = total - high.astype(F32)
    mid = left.astype(BF)
    low = (left - mid.astype(F32)).astype(BF)
    return dot(high, spread_groups) + dot(mid, spread_groups) + dot(low, spread_groups)


def silu(u):
    half = 0.5 * u
    return half + half * jnp.tanh(half)


def block_ones():
    same = (iota((CH, CH), 0) // 16) == (iota((CH, CH), 1) // 16)
    return jnp.where(same, 1.0 / 256.0, 0.0).astype(BF)


def input_weights(w_in_ref):
    return jnp.concatenate(
        [w_in_ref[a, :128, :] for a in range(3)]
        + [w_in_ref[a, 128:144, :] for a in range(3)]
        + [jnp.zeros((80, CH), BF)],
        axis=0,
    )


def normalised(read, write, rows, groups, gain, shift):
    total = jnp.zeros((rows, CH), F32)
    for c in range(CELLS):
        total = total + read(c).astype(F32)
    center = group_mean(total, groups)
    square = jnp.zeros((rows, CH), F32)
    for c in range(CELLS):
        off = read(c).astype(F32) - center
        square = square + off * off
    scale = lax.rsqrt(group_mean(square, groups) + EPSILON) * gain
    for c in range(CELLS):
        u = (read(c).astype(F32) - center) * scale + shift
        write(c, silu(u).astype(BF))


def patches(frames, rows, sel, rest):
    shifted = [frames[a * 32:a * 32 + rows] for a in range(3)]
    return (
        dot(frames, sel[...]).astype(BF),
        dot(jnp.concatenate(shifted, axis=1), rest[...]).astype(BF),
    )


def features_of(found, rows, w_cat, bias, live, write, groups):
    taps, rest = found
    for cells in groups:
        depth = 512 if cells[0] in REST_CELLS else 384
        left = []
        for c in cells:
            block = [taps[a * 32:a * 32 + rows, c * 128:c * 128 + 128] for a in range(3)]
            if depth == 512:
                at = REST_CELLS.index(c)
                block.append(rest[:, at * 128:at * 128 + 128])
            left.append(jnp.concatenate(block, axis=1))
        made = dot(jnp.concatenate(left, axis=0), w_cat[:depth])
        for i, c in enumerate(cells):
            write(c, ((made[i * rows:(i + 1) * rows] + bias) * live).astype(BF))


def lane_halves(pick_row, pick_col_of, source):
    return jnp.concatenate(
        [dot(onehot(pick_row == pick_col_of(half)), source) for half in range(2)], axis=1
    )


def front_kernel(
    latent_hbm, owner_hbm, next_hbm, cache_hbm, hist_hbm, w_in_hbm, bias_hbm, gain_hbm,
    shift_hbm, sel_hbm, rest_hbm,
    trans_hbm, feat_hbm, live_hbm, later_hbm,
    latent, owner, nexts, cache, hist, w_in, bias_v, gain_v, shift_v, sel, rest,
    send_a, recv_a, send_b, recv_x, recv_e, feat, trans, live_v,
    sem_in, sem_out, sem_sa, sem_ra, sem_sx, sem_rx, sem_se, sem_re,
):
    g = lax.axis_index("gen")
    d = lax.axis_index("dec")
    x, e = d // 8, d % 8
    gens = [lax.rem(g + i, 4) for i in (1, 2, 3)]
    xs = [lax.rem(x + i, 4) for i in (1, 2, 3)]
    es = [lax.rem(e + i, 8) for i in range(1, 8)]
    mesh_ids = pl.DeviceIdType.MESH
    barrier = pltpu.get_barrier_semaphore()
    peers = [{"gen": p} for p in gens]
    peers += [{"dec": p * 8 + e} for p in xs]
    peers += [{"dec": x * 8 + p} for p in es]
    for peer in peers:
        pl.semaphore_signal(barrier, inc=1, device_id=peer, device_id_type=mesh_ids)

    loads = []
    for i, (src, dst) in enumerate((
        (latent_hbm, latent), (owner_hbm, owner), (next_hbm, nexts), (cache_hbm, cache),
        (hist_hbm, hist), (sel_hbm, sel), (rest_hbm, rest), (w_in_hbm, w_in),
        (bias_hbm, bias_v), (gain_hbm, gain_v), (shift_hbm, shift_v),
    )):
        load = pltpu.make_async_copy(src, dst, sem_in.at[i])
        load.start()
        loads.append(load)

    groups = block_ones()
    turn = onehot(iota((64, 64), 1) == (iota((64, 64), 0) % 32) * 2 + iota((64, 64), 0) // 32)

    loads[0].wait()
    loads[1].wait()
    loads[2].wait()
    codes = ranked_codes(owner[...].astype(F32), GEN, CAP_L)
    lane = iota((GEN, 256), 1)
    clip_at = jnp.where(lane < 192, (lane % 96) // 4, -1)
    lanes = spread(codes, clip_at, GEN, 256)
    row = iota((N_GEN * MSG_A, 256), 0)
    col = iota((N_GEN * MSG_A, 256), 1)
    named = ((row // MSG_A) * CAP_L + (row % MSG_A) // PART).astype(F32) == lanes
    pick = named & ((row % PART) == (col % 4) * 2 + col // 96) & (col < 192)
    present = jnp.sum(jnp.where(pick, 1.0, 0.0), axis=1, keepdims=True)
    rows = latent[...].reshape(GEN * FR, LAT * CELLS)
    rows = jnp.concatenate([rows[:, :128], rows[:, 128:], jnp.zeros((64, 128), BF)], axis=0)
    ready = jnp.where(present > 0.5, dot(onehot(pick), rows), DEAD)
    send_a[...] = ready.astype(BF).reshape(send_a.shape)
    recv_a[g] = send_a[g]

    pl.semaphore_wait(barrier, len(peers))

    def copy_a(target, landed):
        return pltpu.make_async_remote_copy(
            src_ref=send_a.at[target], dst_ref=recv_a.at[landed],
            send_sem=sem_sa.at[target], recv_sem=sem_ra.at[landed],
            device_id={"gen": target}, device_id_type=mesh_ids,
        )

    for p in gens:
        copy_a(p, g).start()

    codes_b = ranked_codes(nexts[...].astype(F32), DSLOTS, CAP_C)
    lane_b = iota((DSLOTS, 256), 1)
    lanes_b = spread(codes_b, lane_b // PART, DSLOTS, 256)
    row_b = iota((N_DEC * MSG_B, 256), 0)
    col_b = iota((N_DEC * MSG_B, 256), 1)
    pick_b = ((row_b // PART).astype(F32) == lanes_b) & ((row_b % PART) == (col_b % PART))
    filled = jnp.sum(jnp.where(pick_b, 1.0, 0.0), axis=1, keepdims=True)
    pick_b = onehot(pick_b)
    loads[4].wait()
    loads[3].wait()
    for load in loads[5:]:
        load.wait()
    w_cat = input_weights(w_in)
    bias = bias_v[...].reshape(1, CH)
    gain = gain_v[...].reshape(1, CH)
    shift = shift_v[...].reshape(1, CH)
    cached = dot(turn, cache[...].reshape(64, 256)).astype(BF)

    for p in gens:
        copy_a(p, p).wait_recv()
    got = recv_a[...].reshape(N_GEN * MSG_A, 128)
    messages = jnp.where(filled > 0.5, dot(pick_b, got), EMPTY)
    send_b[...] = messages.astype(BF).reshape(send_b.shape)

    def copy_x(target, landed):
        return pltpu.make_async_remote_copy(
            src_ref=send_b.at[target], dst_ref=recv_x.at[landed],
            send_sem=sem_sx.at[target], recv_sem=sem_rx.at[landed],
            device_id={"dec": target * 8 + e}, device_id_type=mesh_ids,
        )

    def copy_e(target, landed):
        return pltpu.make_async_remote_copy(
            src_ref=recv_x.at[:, target], dst_ref=recv_e.at[landed],
            send_sem=sem_se.at[target], recv_sem=sem_re.at[landed],
            device_id={"dec": x * 8 + target}, device_id_type=mesh_ids,
        )

    for p in xs:
        copy_x(p, x).start()
    recv_x[x] = send_b[x]

    r128 = iota((128, 256), 0)
    placed = lane_halves(
        iota((128, 256), 1), lambda half: (r128 % 32) * PART + (r128 // 32) * 2 + half, got
    )
    live = jnp.where(placed[:, :1] < 32.0, 1.0, 0.0)
    live_v[...] = jnp.broadcast_to(live[:64], (64, 128))
    fresh = jnp.where(placed > 32.0, 0.0, placed).astype(BF)
    found = patches(jnp.concatenate([cached, fresh], axis=0), 128, sel, rest)

    def put_feat(cell, value):
        feat[cell] = value

    features_of(found, 128, w_cat, bias, live, put_feat, (REST_CELLS,))

    features_of(found, 128, w_cat, bias, live, put_feat, (PLAIN_CELLS,))

    for p in xs:
        copy_x(p, p).wait_recv()
    for p in es:
        copy_e(p, e).start()
    recv_e[e] = recv_x[:, e]
    outs = [pltpu.make_async_copy(feat, feat_hbm, sem_out.at[0]),
            pltpu.make_async_copy(live_v, live_hbm, sem_out.at[1])]
    for out in outs:
        out.start()

    total = jnp.zeros((128, CH), F32)
    for cell in range(CELLS):
        total = total + feat[cell].astype(F32)
    center = group_mean(total, groups)
    square = jnp.zeros((128, CH), F32)
    for cell in range(CELLS):
        off = feat[cell].astype(F32) - center
        square = square + off * off
    scale = lax.rsqrt(group_mean(square, groups) + EPSILON) * gain

    for cell in range(CELLS):
        u = (feat[cell].astype(F32) - center) * scale + shift
        act = silu(u).astype(BF)
        old = dot(turn, hist[:, :, cell * CH:(cell + 1) * CH].reshape(64, CH)).astype(BF)
        q = [old[:32], old[32:]] + [act[t * 32:t * 32 + 32] for t in range(4)]
        for tile in range(2):
            d0, d1, d2, d3 = q[2 * tile:2 * tile + 4]
            at = slice(tile * 32, tile * 32 + 32)
            trans[0, cell, at] = d0 - d2
            trans[1, cell, at] = d1 + d2
            trans[2, cell, at] = d2 - d1
            trans[3, cell, at] = d1 - d3
        if cell % 2 == 1:
            part = pl.ds(cell - 1, 2)
            out = pltpu.make_async_copy(
                trans.at[:, part], trans_hbm.at[:, part], sem_out.at[2 + cell // 2]
            )
            out.start()
            outs.append(out)

    for p in es:
        copy_e(p, p).wait_recv()
    out = pltpu.make_async_copy(recv_e, later_hbm, sem_out.at[10])
    out.start()
    outs.append(out)
    for p in gens:
        copy_a(p, g).wait_send()
    for p in xs:
        copy_x(p, x).wait_send()
    for p in es:
        copy_e(p, e).wait_send()
    for out in outs:
        out.wait()


def front(latent, owner, nexts, cache_latent, cache_act, weight_in, bias_in, gain, shift, sel, rest):
    hbm = pl.BlockSpec(memory_space=pltpu.HBM)
    wide = CELLS * CH
    dma = pltpu.SemaphoreType.DMA
    return pl.pallas_call(
        front_kernel,
        out_shape=(
            jax.ShapeDtypeStruct((4, CELLS, 64, CH), BF),
            jax.ShapeDtypeStruct((CELLS, 128, CH), BF),
            jax.ShapeDtypeStruct((64, 128), F32),
            jax.ShapeDtypeStruct((8, 4, MSG_B, 128), BF),
        ),
        in_specs=[hbm] * 11,
        out_specs=(hbm,) * 4,
        scratch_shapes=[
            pltpu.VMEM((GEN, FR, LAT * CELLS), BF),
            pltpu.VMEM((1, GEN), I32),
            pltpu.VMEM((1, DSLOTS), I32),
            pltpu.VMEM((DSLOTS, 2, LAT * CELLS), BF),
            pltpu.VMEM((DSLOTS, 2, wide), BF),
            pltpu.VMEM((3, 9 * LAT, CH), BF),
            pltpu.VMEM((CH,), F32),
            pltpu.VMEM((CH,), F32),
            pltpu.VMEM((CH,), F32),
            pltpu.VMEM(sel.shape, BF),
            pltpu.VMEM(rest.shape, BF),
            pltpu.VMEM((N_GEN, MSG_A, 128), BF),
            pltpu.VMEM((N_GEN, MSG_A, 128), BF),
            pltpu.VMEM((4, 8, MSG_B, 128), BF),
            pltpu.VMEM((4, 8, MSG_B, 128), BF),
            pltpu.VMEM((8, 4, MSG_B, 128), BF),
            pltpu.VMEM((CELLS, 128, CH), BF),
            pltpu.VMEM((4, CELLS, 64, CH), BF),
            pltpu.VMEM((64, 128), F32),
            dma((11,)), dma((11,)), dma((4,)), dma((4,)), dma((4,)), dma((4,)), dma((8,)), dma((8,)),
        ],
        compiler_params=pltpu.CompilerParams(
            collective_id=0, has_side_effects=True, vmem_limit_bytes=LIM
        ),
        name="front",
    )(latent, owner, nexts, cache_latent, cache_act, weight_in, bias_in, gain, shift, sel, rest)


def decode_kernel(
    trans_hbm, feat_hbm, live_hbm, later_hbm, w_in_hbm, bias_hbm, gain_hbm, shift_hbm,
    bias_mid_hbm, sel_hbm, rest_hbm, w_mid_hbm,
    feat_out_hbm, conv_hbm, nlat_hbm, nact_hbm,
    trans, feat, live_v, later_v, w_in, bias_v, gain_v, shift_v, bias_mid_v, sel, rest, w_mid,
    sums, mixed, wide_out, nact_out, nlat_out,
    sem_in, sem_w, sem_out,
):
    loads = [
        pltpu.make_async_copy(src, dst, sem_in.at[i])
        for i, (src, dst) in enumerate((
            (later_hbm, later_v), (sel_hbm, sel), (rest_hbm, rest), (w_in_hbm, w_in),
            (bias_hbm, bias_v), (gain_hbm, gain_v), (shift_hbm, shift_v),
            (bias_mid_hbm, bias_mid_v), (live_hbm, live_v), (feat_hbm, feat),
            (trans_hbm, trans),
        ))
    ]
    for load in loads:
        load.start()
    w_copies = [
        pltpu.make_async_copy(
            w_mid_hbm.at[:, pl.ds(tap * CH, CH), :], w_mid.at[at % (AHEAD + 1)], sem_w.at[at]
        )
        for at, tap in enumerate(TAPS)
    ]
    for copy in w_copies[:AHEAD]:
        copy.start()

    groups = block_ones()
    loads[0].wait()
    got = later_v[...].reshape(N_DEC * MSG_B, 128)
    flags = lax.dot_general(
        onehot(iota((8, 128), 1) == 0), got, (((1,), (1,)), ((), ())),
        preferred_element_type=F32,
    )
    flags = onehot(flags < 100.0)

    def entry_of(row):
        return (((row // 16) % 4) * 8 + row // 64) * CAP_C + (row // PART) % CAP_C

    big = iota((512, 128), 0)
    held = dot(flags, onehot((big % PART == 0) & (entry_of(big) == iota((512, 128), 1))))
    before = onehot(iota((128, 128), 0) < iota((128, 128), 1))
    place = dot(held.astype(BF), before)
    take = onehot((held[:1] > 0.5) & (place[:1] == iota((32, 128), 0).astype(F32)))
    lane = iota((128, 512), 1)
    entry = entry_of(lane) == iota((128, 512), 0)
    take = dot(take, onehot(entry)).astype(BF)
    wide = jnp.concatenate([take] * 4, axis=0)
    kind = iota((128, 512), 0) // 32
    halves = [
        dot(jnp.where(iota((128, 512), 1) % PART == kind * 2 + half, wide, 0), got)
        for half in range(2)
    ]
    moved = jnp.concatenate(halves, axis=1)
    live_next = jnp.where(moved[:64, :1] < 32.0, 1.0, 0.0)
    fresh = jnp.where(moved > 32.0, 0.0, moved).astype(BF)
    pair = onehot(iota((64, 64), 1) == (iota((64, 64), 0) % 2) * 32 + iota((64, 64), 0) // 2)
    nlat_out[...] = dot(pair, fresh[64:]).astype(BF).reshape(32, 2, 256)
    outs = [pltpu.make_async_copy(nlat_out, nlat_hbm, sem_out.at[0])]
    outs[0].start()

    for load in loads[1:9]:
        load.wait()
    w_cat = input_weights(w_in)
    bias = bias_v[...].reshape(1, CH)
    gain = gain_v[...].reshape(1, CH)
    shift = shift_v[...].reshape(1, CH)
    bias_mid = bias_mid_v[...].reshape(1, CH)

    def put_mixed(cell, value):
        mixed[cell] = value

    features_of(patches(fresh, 64, sel, rest), 64, w_cat, bias, live_next, put_mixed,
                (REST_CELLS, PLAIN_CELLS))

    order = onehot(
        iota((128, 128), 1) == (iota((128, 128), 0) % 4) * 32 + iota((128, 128), 0) // 4
    )

    def put_next(cell, value):
        turned = dot(order, feat[cell]).astype(BF).reshape(32, 4, CH)
        wide_out[:, :, cell * CH:(cell + 1) * CH] = turned
        value = (value.astype(F32) * live_next).astype(BF)
        nact_out[:, :, cell * CH:(cell + 1) * CH] = dot(pair, value).astype(BF).reshape(32, 2, CH)

    loads[9].wait()
    normalised(lambda cell: mixed[cell], put_next, 64, groups, gain, shift)
    out = pltpu.make_async_copy(nact_out, nact_hbm, sem_out.at[1])
    out.start()
    outs.append(out)

    feat_copy = pltpu.make_async_copy(wide_out, feat_out_hbm, sem_out.at[2])
    feat_copy.start()

    loads[10].wait()
    for at, tap in enumerate(TAPS):
        if at + AHEAD < len(TAPS):
            w_copies[at + AHEAD].start()
        w_copies[at].wait()
        here = at % (AHEAD + 1)
        g0 = w_mid[here, 0].astype(F32)
        g1 = w_mid[here, 1].astype(F32)
        g2 = w_mid[here, 2].astype(F32)
        ends = g0 + g2
        weights = [
            w_mid[here, 0], ((ends + g1) * 0.5).astype(BF), ((ends - g1) * 0.5).astype(BF),
            w_mid[here, 2],
        ]
        pairs = tap_cells(tap)
        for j in range(4):
            left = jnp.concatenate([trans[j, source] for _, source in pairs], axis=0)
            made = dot(left, weights[j])
            for i, (cell, _) in enumerate(pairs):
                piece = made[i * 64:(i + 1) * 64]
                if at == 0:
                    sums[j, cell] = piece
                else:
                    sums[j, cell] += piece

    r128 = iota((128, 128), 0)
    back = onehot(iota((128, 128), 1) == (r128 % 2) * 64 + ((r128 % 4) // 2) * 32 + r128 // 4)
    keep = live_v[...][:, :1]
    feat_copy.wait()
    for cell in range(CELLS):
        both = sums[1, cell] + sums[2, cell]
        apart = sums[1, cell] - sums[2, cell]
        even = ((sums[0, cell] + both + bias_mid) * keep).astype(BF)
        odd = ((apart - sums[3, cell] + bias_mid) * keep).astype(BF)
        turned = dot(back, jnp.concatenate([even, odd], axis=0)).astype(BF)
        wide_out[:, :, cell * CH:(cell + 1) * CH] = turned.reshape(32, 4, CH)
        if cell % 2 == 1:
            lanes = pl.ds((cell - 1) * CH, 2 * CH)
            out = pltpu.make_async_copy(
                wide_out.at[:, :, lanes], conv_hbm.at[:, :, lanes], sem_out.at[3 + cell // 2]
            )
            out.start()
            outs.append(out)
    for out in outs:
        out.wait()


def decode(trans, feat, live, later, weight_in, bias_in, gain, shift, bias_mid, sel, rest,
           weight_mid):
    hbm = pl.BlockSpec(memory_space=pltpu.HBM)
    wide = CELLS * CH
    dma = pltpu.SemaphoreType.DMA
    return pl.pallas_call(
        decode_kernel,
        out_shape=(
            jax.ShapeDtypeStruct((DSLOTS, FR, wide), BF),
            jax.ShapeDtypeStruct((DSLOTS, FR, wide), BF),
            jax.ShapeDtypeStruct((DSLOTS, 2, LAT * CELLS), BF),
            jax.ShapeDtypeStruct((DSLOTS, 2, wide), BF),
        ),
        in_specs=[hbm] * 12,
        out_specs=(hbm,) * 4,
        scratch_shapes=[
            pltpu.VMEM((4, CELLS, 64, CH), BF),
            pltpu.VMEM((CELLS, 128, CH), BF),
            pltpu.VMEM((64, 128), F32),
            pltpu.VMEM((8, 4, MSG_B, 128), BF),
            pltpu.VMEM((3, 9 * LAT, CH), BF),
            pltpu.VMEM((CH,), F32),
            pltpu.VMEM((CH,), F32),
            pltpu.VMEM((CH,), F32),
            pltpu.VMEM((CH,), F32),
            pltpu.VMEM(sel.shape, BF),
            pltpu.VMEM(rest.shape, BF),
            pltpu.VMEM((AHEAD + 1, 3, CH, CH), BF),
            pltpu.VMEM((4, CELLS, 64, CH), F32),
            pltpu.VMEM((CELLS, 64, CH), BF),
            pltpu.VMEM((DSLOTS, FR, wide), BF),
            pltpu.VMEM((DSLOTS, 2, wide), BF),
            pltpu.VMEM((DSLOTS, 2, LAT * CELLS), BF),
            dma((11,)), dma((9,)), dma((11,)),
        ],
        compiler_params=pltpu.CompilerParams(vmem_limit_bytes=LIM),
        name="decode",
    )(trans, feat, live, later, weight_in, bias_in, gain, shift, bias_mid, sel, rest, weight_mid)


def shards(latent, latent_owner, next_owner, cache_latent, cache_act, weight_in, bias_in,
           norm_gain, norm_shift, weight_mid, bias_mid):
    sel, rest = patch_selectors()
    made = front(
        latent, latent_owner.reshape(1, GEN), next_owner.reshape(1, DSLOTS), cache_latent,
        cache_act, weight_in, bias_in, norm_gain, norm_shift, sel, rest,
    )
    return decode(*made, weight_in, bias_in, norm_gain, norm_shift, bias_mid, sel, rest, weight_mid)


def solution(mesh):
    both = ("gen", "dec")
    in_specs = (
        P(both, None, None), P(both, None), P(both), P(both, None, None), P(both, None, None),
        P(), P(), P(), P(), P(), P(),
    )
    out_specs = (P(both, None, None),) * 4
    return jax.shard_map(shards, mesh=mesh, in_specs=in_specs, out_specs=out_specs, check_vma=False)
```

```python
import functools

import jax
import jax.numpy as jnp
import numpy as np
from jax import lax
from jax.experimental import pallas as pl
from jax.experimental.pallas import tpu as pltpu
from jax.sharding import PartitionSpec as P

BF = jnp.bfloat16
F32 = jnp.float32
I32 = jnp.int32

N_GEN, N_DEC = 4, 32
GEN, CAP_L, DSLOTS, CAP_C = 24, 8, 32, 2
FR, CELLS, HT, WT, LAT, CH = 4, 16, 4, 4, 16, 512
PART = 8
MSG_A = CAP_L * PART
MSG_B = CAP_C * PART
DEAD, EMPTY = 64.0, 128.0
EPSILON = 1e-06

AHEAD = 3
LIM = 65400 << 10
TAPS = [4, 1, 3, 5, 7, 0, 2, 6, 8]
REST_CELLS = [y * WT + x for y in range(3) for x in range(3)]
PLAIN_CELLS = [c for c in range(CELLS) if c not in REST_CELLS]


def tap_cells(tap):
    dy, dx = tap // 3 - 1, tap % 3 - 1
    pairs = []
    for y in range(HT):
        for x in range(WT):
            if 0 <= y + dy < HT and 0 <= x + dx < WT:
                pairs.append((y * WT + x, (y + dy) * WT + x + dx))
    return pairs


def patch_selectors():
    first = np.zeros((LAT * CELLS, CELLS * 128), np.float32)
    for tap in range(8):
        for cell, source in tap_cells(tap):
            for e in range(LAT):
                first[e * CELLS + source, cell * 128 + tap * LAT + e] = 1
    rest = np.zeros((3 * LAT * CELLS, len(REST_CELLS) * 128), np.float32)
    for cell, source in tap_cells(8):
        at = REST_CELLS.index(cell)
        for a in range(3):
            for e in range(LAT):
                rest[a * 256 + e * CELLS + source, at * 128 + a * LAT + e] = 1
    return jnp.asarray(first, BF), jnp.asarray(rest, BF)


def dot(a, b):
    return jnp.dot(a, b, preferred_element_type=F32)


def iota(shape, dim):
    return lax.broadcasted_iota(I32, shape, dim)


def onehot(mask):
    return jnp.where(mask, 1.0, 0.0).astype(BF)


def ranked_codes(row, length, per):
    sub = iota((length, length), 0)
    lane = iota((length, length), 1)
    wide = jnp.broadcast_to(row, (length, length))
    col = jnp.sum(jnp.where(sub == lane, wide, 0.0), axis=1, keepdims=True)
    same = (wide == col) & (lane < sub)
    rank = jnp.sum(jnp.where(same, 1.0, 0.0), axis=1, keepdims=True)
    return col * per + rank


def spread(codes, where_to, length, width):
    hit = iota((length, width), 0) == where_to
    found = jnp.sum(jnp.where(hit, codes + 1.0, 0.0), axis=0, keepdims=True)
    return found - 1.0


def group_mean(total, spread_groups):
    high = total.astype(BF)
    left = total - high.astype(F32)
    mid = left.astype(BF)
    low = (left - mid.astype(F32)).astype(BF)
    return dot(high, spread_groups) + dot(mid, spread_groups) + dot(low, spread_groups)


def silu(u):
    half = 0.5 * u
    return half + half * jnp.tanh(half)


def block_ones():
    same = (iota((CH, CH), 0) // 16) == (iota((CH, CH), 1) // 16)
    return jnp.where(same, 1.0 / 256.0, 0.0).astype(BF)


def input_weights(w_in_ref):
    return jnp.concatenate(
        [w_in_ref[a, :128, :] for a in range(3)]
        + [w_in_ref[a, 128:144, :] for a in range(3)]
        + [jnp.zeros((80, CH), BF)],
        axis=0,
    )


def normalised(read, write, rows, groups, gain, shift):
    total = jnp.zeros((rows, CH), F32)
    for c in range(CELLS):
        total = total + read(c).astype(F32)
    center = group_mean(total, groups)
    square = jnp.zeros((rows, CH), F32)
    for c in range(CELLS):
        off = read(c).astype(F32) - center
        square = square + off * off
    scale = lax.rsqrt(group_mean(square, groups) + EPSILON) * gain
    for c in range(CELLS):
        u = (read(c).astype(F32) - center) * scale + shift
        write(c, silu(u).astype(BF))


def patches(frames, rows, sel, rest):
    shifted = [frames[a * 32:a * 32 + rows] for a in range(3)]
    return (
        dot(frames, sel[...]).astype(BF),
        dot(jnp.concatenate(shifted, axis=1), rest[...]).astype(BF),
    )


def features_of(found, rows, w_cat, bias, live, write, groups):
    taps, rest = found
    for cells in groups:
        depth = 512 if cells[0] in REST_CELLS else 384
        left = []
        for c in cells:
            block = [taps[a * 32:a * 32 + rows, c * 128:c * 128 + 128] for a in range(3)]
            if depth == 512:
                at = REST_CELLS.index(c)
                block.append(rest[:, at * 128:at * 128 + 128])
            left.append(jnp.concatenate(block, axis=1))
        made = dot(jnp.concatenate(left, axis=0), w_cat[:depth])
        for i, c in enumerate(cells):
            write(c, ((made[i * rows:(i + 1) * rows] + bias) * live).astype(BF))


def lane_halves(pick_row, pick_col_of, source):
    return jnp.concatenate(
        [dot(onehot(pick_row == pick_col_of(half)), source) for half in range(2)], axis=1
    )


def front_kernel(
    latent_hbm, owner_hbm, next_hbm, cache_hbm, hist_hbm, w_in_hbm, bias_hbm, gain_hbm,
    shift_hbm, sel_hbm, rest_hbm,
    trans_hbm, feat_hbm, live_hbm, later_hbm,
    latent, owner, nexts, cache, hist, w_in, bias_v, gain_v, shift_v, sel, rest,
    send_a, recv_a, send_b, recv_x, recv_e, feat, trans, live_v,
    sem_in, sem_out, sem_sa, sem_ra, sem_sx, sem_rx, sem_se, sem_re,
):
    g = lax.axis_index("gen")
    d = lax.axis_index("dec")
    x, e = d // 8, d % 8
    gens = [lax.rem(g + i, 4) for i in (1, 2, 3)]
    xs = [lax.rem(x + i, 4) for i in (1, 2, 3)]
    es = [lax.rem(e + i, 8) for i in range(1, 8)]
    mesh_ids = pl.DeviceIdType.MESH
    barrier = pltpu.get_barrier_semaphore()
    peers = [{"gen": p} for p in gens]
    peers += [{"dec": p * 8 + e} for p in xs]
    peers += [{"dec": x * 8 + p} for p in es]
    for peer in peers:
        pl.semaphore_signal(barrier, inc=1, device_id=peer, device_id_type=mesh_ids)

    loads = []
    for i, (src, dst) in enumerate((
        (latent_hbm, latent), (owner_hbm, owner), (next_hbm, nexts), (cache_hbm, cache),
        (hist_hbm, hist), (sel_hbm, sel), (rest_hbm, rest), (w_in_hbm, w_in),
        (bias_hbm, bias_v), (gain_hbm, gain_v), (shift_hbm, shift_v),
    )):
        load = pltpu.make_async_copy(src, dst, sem_in.at[i])
        load.start()
        loads.append(load)

    groups = block_ones()
    turn = onehot(iota((64, 64), 1) == (iota((64, 64), 0) % 32) * 2 + iota((64, 64), 0) // 32)

    loads[0].wait()
    loads[1].wait()
    loads[2].wait()
    codes = ranked_codes(owner[...].astype(F32), GEN, CAP_L)
    lane = iota((GEN, 256), 1)
    clip_at = jnp.where(lane < 192, (lane % 96) // 4, -1)
    lanes = spread(codes, clip_at, GEN, 256)
    row = iota((N_GEN * MSG_A, 256), 0)
    col = iota((N_GEN * MSG_A, 256), 1)
    named = ((row // MSG_A) * CAP_L + (row % MSG_A) // PART).astype(F32) == lanes
    pick = named & ((row % PART) == (col % 4) * 2 + col // 96) & (col < 192)
    present = jnp.sum(jnp.where(pick, 1.0, 0.0), axis=1, keepdims=True)
    rows = latent[...].reshape(GEN * FR, LAT * CELLS)
    rows = jnp.concatenate([rows[:, :128], rows[:, 128:], jnp.zeros((64, 128), BF)], axis=0)
    ready = jnp.where(present > 0.5, dot(onehot(pick), rows), DEAD)
    send_a[...] = ready.astype(BF).reshape(send_a.shape)
    recv_a[g] = send_a[g]

    pl.semaphore_wait(barrier, len(peers))

    def copy_a(target, landed):
        return pltpu.make_async_remote_copy(
            src_ref=send_a.at[target], dst_ref=recv_a.at[landed],
            send_sem=sem_sa.at[target], recv_sem=sem_ra.at[landed],
            device_id={"gen": target}, device_id_type=mesh_ids,
        )

    for p in gens:
        copy_a(p, g).start()

    codes_b = ranked_codes(nexts[...].astype(F32), DSLOTS, CAP_C)
    lane_b = iota((DSLOTS, 256), 1)
    lanes_b = spread(codes_b, lane_b // PART, DSLOTS, 256)
    row_b = iota((N_DEC * MSG_B, 256), 0)
    col_b = iota((N_DEC * MSG_B, 256), 1)
    pick_b = ((row_b // PART).astype(F32) == lanes_b) & ((row_b % PART) == (col_b % PART))
    filled = jnp.sum(jnp.where(pick_b, 1.0, 0.0), axis=1, keepdims=True)
    pick_b = onehot(pick_b)
    loads[4].wait()
    loads[3].wait()
    for load in loads[5:]:
        load.wait()
    w_cat = input_weights(w_in)
    bias = bias_v[...].reshape(1, CH)
    gain = gain_v[...].reshape(1, CH)
    shift = shift_v[...].reshape(1, CH)
    cached = dot(turn, cache[...].reshape(64, 256)).astype(BF)

    for p in gens:
        copy_a(p, p).wait_recv()
    got = recv_a[...].reshape(N_GEN * MSG_A, 128)
    messages = jnp.where(filled > 0.5, dot(pick_b, got), EMPTY)
    send_b[...] = messages.astype(BF).reshape(send_b.shape)

    def copy_x(target, landed):
        return pltpu.make_async_remote_copy(
            src_ref=send_b.at[target], dst_ref=recv_x.at[landed],
            send_sem=sem_sx.at[target], recv_sem=sem_rx.at[landed],
            device_id={"dec": target * 8 + e}, device_id_type=mesh_ids,
        )

    def copy_e(target, landed):
        return pltpu.make_async_remote_copy(
            src_ref=recv_x.at[:, target], dst_ref=recv_e.at[landed],
            send_sem=sem_se.at[target], recv_sem=sem_re.at[landed],
            device_id={"dec": x * 8 + target}, device_id_type=mesh_ids,
        )

    for p in xs:
        copy_x(p, x).start()
    recv_x[x] = send_b[x]

    r128 = iota((128, 256), 0)
    placed = lane_halves(
        iota((128, 256), 1), lambda half: (r128 % 32) * PART + (r128 // 32) * 2 + half, got
    )
    live = jnp.where(placed[:, :1] < 32.0, 1.0, 0.0)
    live_v[...] = jnp.broadcast_to(live[:64], (64, 128))
    fresh = jnp.where(placed > 32.0, 0.0, placed).astype(BF)
    found = patches(jnp.concatenate([cached, fresh], axis=0), 128, sel, rest)

    total = [jnp.zeros((128, CH), F32)]

    def put_feat(cell, value):
        feat[cell] = value
        total[0] = total[0] + value.astype(F32)

    features_of(found, 128, w_cat, bias, live, put_feat, (REST_CELLS,))

    features_of(found, 128, w_cat, bias, live, put_feat, (PLAIN_CELLS,))

    for p in xs:
        copy_x(p, p).wait_recv()
    for p in es:
        copy_e(p, e).start()
    recv_e[e] = recv_x[:, e]
    outs = [pltpu.make_async_copy(feat, feat_hbm, sem_out.at[0]),
            pltpu.make_async_copy(live_v, live_hbm, sem_out.at[1])]
    for out in outs:
        out.start()

    center = group_mean(total[0], groups)
    square = jnp.zeros((128, CH), F32)
    for cell in range(CELLS):
        off = feat[cell].astype(F32) - center
        square = square + off * off
    scale = lax.rsqrt(group_mean(square, groups) + EPSILON) * gain

    for cell in range(CELLS):
        u = (feat[cell].astype(F32) - center) * scale + shift
        act = silu(u).astype(BF)
        old = dot(turn, hist[:, :, cell * CH:(cell + 1) * CH].reshape(64, CH)).astype(BF)
        q = [old[:32], old[32:]] + [act[t * 32:t * 32 + 32] for t in range(4)]
        for tile in range(2):
            d0, d1, d2, d3 = q[2 * tile:2 * tile + 4]
            at = slice(tile * 32, tile * 32 + 32)
            trans[0, cell, at] = d0 - d2
            trans[1, cell, at] = d1 + d2
            trans[2, cell, at] = d2 - d1
            trans[3, cell, at] = d1 - d3
        if cell % 2 == 1:
            part = pl.ds(cell - 1, 2)
            out = pltpu.make_async_copy(
                trans.at[:, part], trans_hbm.at[:, part], sem_out.at[2 + cell // 2]
            )
            out.start()
            outs.append(out)

    for p in es:
        copy_e(p, p).wait_recv()
    out = pltpu.make_async_copy(recv_e, later_hbm, sem_out.at[10])
    out.start()
    outs.append(out)
    for p in gens:
        copy_a(p, g).wait_send()
    for p in xs:
        copy_x(p, x).wait_send()
    for p in es:
        copy_e(p, e).wait_send()
    for out in outs:
        out.wait()


def front(latent, owner, nexts, cache_latent, cache_act, weight_in, bias_in, gain, shift, sel, rest):
    hbm = pl.BlockSpec(memory_space=pltpu.HBM)
    wide = CELLS * CH
    dma = pltpu.SemaphoreType.DMA
    return pl.pallas_call(
        front_kernel,
        out_shape=(
            jax.ShapeDtypeStruct((4, CELLS, 64, CH), BF),
            jax.ShapeDtypeStruct((CELLS, 128, CH), BF),
            jax.ShapeDtypeStruct((64, 128), F32),
            jax.ShapeDtypeStruct((8, 4, MSG_B, 128), BF),
        ),
        in_specs=[hbm] * 11,
        out_specs=(hbm,) * 4,
        scratch_shapes=[
            pltpu.VMEM((GEN, FR, LAT * CELLS), BF),
            pltpu.VMEM((1, GEN), I32),
            pltpu.VMEM((1, DSLOTS), I32),
            pltpu.VMEM((DSLOTS, 2, LAT * CELLS), BF),
            pltpu.VMEM((DSLOTS, 2, wide), BF),
            pltpu.VMEM((3, 9 * LAT, CH), BF),
            pltpu.VMEM((CH,), F32),
            pltpu.VMEM((CH,), F32),
            pltpu.VMEM((CH,), F32),
            pltpu.VMEM(sel.shape, BF),
            pltpu.VMEM(rest.shape, BF),
            pltpu.VMEM((N_GEN, MSG_A, 128), BF),
            pltpu.VMEM((N_GEN, MSG_A, 128), BF),
            pltpu.VMEM((4, 8, MSG_B, 128), BF),
            pltpu.VMEM((4, 8, MSG_B, 128), BF),
            pltpu.VMEM((8, 4, MSG_B, 128), BF),
            pltpu.VMEM((CELLS, 128, CH), BF),
            pltpu.VMEM((4, CELLS, 64, CH), BF),
            pltpu.VMEM((64, 128), F32),
            dma((11,)), dma((11,)), dma((4,)), dma((4,)), dma((4,)), dma((4,)), dma((8,)), dma((8,)),
        ],
        compiler_params=pltpu.CompilerParams(
            collective_id=0, has_side_effects=True, vmem_limit_bytes=LIM
        ),
        name="front",
    )(latent, owner, nexts, cache_latent, cache_act, weight_in, bias_in, gain, shift, sel, rest)


def decode_kernel(
    trans_hbm, feat_hbm, live_hbm, later_hbm, w_in_hbm, bias_hbm, gain_hbm, shift_hbm,
    bias_mid_hbm, sel_hbm, rest_hbm, w_mid_hbm,
    feat_out_hbm, conv_hbm, nlat_hbm, nact_hbm,
    trans, feat, live_v, later_v, w_in, bias_v, gain_v, shift_v, bias_mid_v, sel, rest, w_mid,
    sums, mixed, wide_out, nact_out, nlat_out,
    sem_in, sem_w, sem_out,
):
    loads = [
        pltpu.make_async_copy(src, dst, sem_in.at[i])
        for i, (src, dst) in enumerate((
            (later_hbm, later_v), (sel_hbm, sel), (rest_hbm, rest), (w_in_hbm, w_in),
            (bias_hbm, bias_v), (gain_hbm, gain_v), (shift_hbm, shift_v),
            (bias_mid_hbm, bias_mid_v), (live_hbm, live_v), (feat_hbm, feat),
            (trans_hbm, trans),
        ))
    ]
    for load in loads:
        load.start()
    w_copies = [
        pltpu.make_async_copy(
            w_mid_hbm.at[:, pl.ds(tap * CH, CH), :], w_mid.at[at % (AHEAD + 1)], sem_w.at[at]
        )
        for at, tap in enumerate(TAPS)
    ]
    for copy in w_copies[:AHEAD]:
        copy.start()

    groups = block_ones()
    loads[0].wait()
    got = later_v[...].reshape(N_DEC * MSG_B, 128)
    flags = lax.dot_general(
        onehot(iota((8, 128), 1) == 0), got, (((1,), (1,)), ((), ())),
        preferred_element_type=F32,
    )
    flags = onehot(flags < 100.0)

    def entry_of(row):
        return (((row // 16) % 4) * 8 + row // 64) * CAP_C + (row // PART) % CAP_C

    big = iota((512, 128), 0)
    held = dot(flags, onehot((big % PART == 0) & (entry_of(big) == iota((512, 128), 1))))
    before = onehot(iota((128, 128), 0) < iota((128, 128), 1))
    place = dot(held.astype(BF), before)
    take = onehot((held[:1] > 0.5) & (place[:1] == iota((32, 128), 0).astype(F32)))
    lane = iota((128, 512), 1)
    entry = entry_of(lane) == iota((128, 512), 0)
    take = dot(take, onehot(entry)).astype(BF)
    wide = jnp.concatenate([take] * 4, axis=0)
    kind = iota((128, 512), 0) // 32
    halves = [
        dot(jnp.where(iota((128, 512), 1) % PART == kind * 2 + half, wide, 0), got)
        for half in range(2)
    ]
    moved = jnp.concatenate(halves, axis=1)
    live_next = jnp.where(moved[:64, :1] < 32.0, 1.0, 0.0)
    fresh = jnp.where(moved > 32.0, 0.0, moved).astype(BF)
    pair = onehot(iota((64, 64), 1) == (iota((64, 64), 0) % 2) * 32 + iota((64, 64), 0) // 2)
    nlat_out[...] = dot(pair, fresh[64:]).astype(BF).reshape(32, 2, 256)
    outs = [pltpu.make_async_copy(nlat_out, nlat_hbm, sem_out.at[0])]
    outs[0].start()

    for load in loads[1:9]:
        load.wait()
    w_cat = input_weights(w_in)
    bias = bias_v[...].reshape(1, CH)
    gain = gain_v[...].reshape(1, CH)
    shift = shift_v[...].reshape(1, CH)
    bias_mid = bias_mid_v[...].reshape(1, CH)

    def put_mixed(cell, value):
        mixed[cell] = value

    features_of(patches(fresh, 64, sel, rest), 64, w_cat, bias, live_next, put_mixed,
                (REST_CELLS, PLAIN_CELLS))

    order = onehot(
        iota((128, 128), 1) == (iota((128, 128), 0) % 4) * 32 + iota((128, 128), 0) // 4
    )

    def put_next(cell, value):
        turned = dot(order, feat[cell]).astype(BF).reshape(32, 4, CH)
        wide_out[:, :, cell * CH:(cell + 1) * CH] = turned
        value = (value.astype(F32) * live_next).astype(BF)
        nact_out[:, :, cell * CH:(cell + 1) * CH] = dot(pair, value).astype(BF).reshape(32, 2, CH)

    loads[9].wait()
    normalised(lambda cell: mixed[cell], put_next, 64, groups, gain, shift)
    out = pltpu.make_async_copy(nact_out, nact_hbm, sem_out.at[1])
    out.start()
    outs.append(out)

    feat_copy = pltpu.make_async_copy(wide_out, feat_out_hbm, sem_out.at[2])
    feat_copy.start()

    loads[10].wait()
    for at, tap in enumerate(TAPS):
        if at + AHEAD < len(TAPS):
            w_copies[at + AHEAD].start()
        w_copies[at].wait()
        here = at % (AHEAD + 1)
        g0 = w_mid[here, 0].astype(F32)
        g1 = w_mid[here, 1].astype(F32)
        g2 = w_mid[here, 2].astype(F32)
        ends = g0 + g2
        weights = [
            w_mid[here, 0], ((ends + g1) * 0.5).astype(BF), ((ends - g1) * 0.5).astype(BF),
            w_mid[here, 2],
        ]
        pairs = tap_cells(tap)
        for j in range(4):
            left = jnp.concatenate([trans[j, source] for _, source in pairs], axis=0)
            made = dot(left, weights[j])
            for i, (cell, _) in enumerate(pairs):
                piece = made[i * 64:(i + 1) * 64]
                if at == 0:
                    sums[j, cell] = piece
                else:
                    sums[j, cell] += piece

    r128 = iota((128, 128), 0)
    back = onehot(iota((128, 128), 1) == (r128 % 2) * 64 + ((r128 % 4) // 2) * 32 + r128 // 4)
    keep = live_v[...][:, :1]
    feat_copy.wait()
    for cell in range(CELLS):
        both = sums[1, cell] + sums[2, cell]
        apart = sums[1, cell] - sums[2, cell]
        even = ((sums[0, cell] + both + bias_mid) * keep).astype(BF)
        odd = ((apart - sums[3, cell] + bias_mid) * keep).astype(BF)
        turned = dot(back, jnp.concatenate([even, odd], axis=0)).astype(BF)
        wide_out[:, :, cell * CH:(cell + 1) * CH] = turned.reshape(32, 4, CH)
        if cell % 2 == 1:
            lanes = pl.ds((cell - 1) * CH, 2 * CH)
            out = pltpu.make_async_copy(
                wide_out.at[:, :, lanes], conv_hbm.at[:, :, lanes], sem_out.at[3 + cell // 2]
            )
            out.start()
            outs.append(out)
    for out in outs:
        out.wait()


def decode(trans, feat, live, later, weight_in, bias_in, gain, shift, bias_mid, sel, rest,
           weight_mid):
    hbm = pl.BlockSpec(memory_space=pltpu.HBM)
    wide = CELLS * CH
    dma = pltpu.SemaphoreType.DMA
    return pl.pallas_call(
        decode_kernel,
        out_shape=(
            jax.ShapeDtypeStruct((DSLOTS, FR, wide), BF),
            jax.ShapeDtypeStruct((DSLOTS, FR, wide), BF),
            jax.ShapeDtypeStruct((DSLOTS, 2, LAT * CELLS), BF),
            jax.ShapeDtypeStruct((DSLOTS, 2, wide), BF),
        ),
        in_specs=[hbm] * 12,
        out_specs=(hbm,) * 4,
        scratch_shapes=[
            pltpu.VMEM((4, CELLS, 64, CH), BF),
            pltpu.VMEM((CELLS, 128, CH), BF),
            pltpu.VMEM((64, 128), F32),
            pltpu.VMEM((8, 4, MSG_B, 128), BF),
            pltpu.VMEM((3, 9 * LAT, CH), BF),
            pltpu.VMEM((CH,), F32),
            pltpu.VMEM((CH,), F32),
            pltpu.VMEM((CH,), F32),
            pltpu.VMEM((CH,), F32),
            pltpu.VMEM(sel.shape, BF),
            pltpu.VMEM(rest.shape, BF),
            pltpu.VMEM((AHEAD + 1, 3, CH, CH), BF),
            pltpu.VMEM((4, CELLS, 64, CH), F32),
            pltpu.VMEM((CELLS, 64, CH), BF),
            pltpu.VMEM((DSLOTS, FR, wide), BF),
            pltpu.VMEM((DSLOTS, 2, wide), BF),
            pltpu.VMEM((DSLOTS, 2, LAT * CELLS), BF),
            dma((11,)), dma((9,)), dma((11,)),
        ],
        compiler_params=pltpu.CompilerParams(vmem_limit_bytes=LIM),
        name="decode",
    )(trans, feat, live, later, weight_in, bias_in, gain, shift, bias_mid, sel, rest, weight_mid)


def shards(latent, latent_owner, next_owner, cache_latent, cache_act, weight_in, bias_in,
           norm_gain, norm_shift, weight_mid, bias_mid):
    sel, rest = patch_selectors()
    made = front(
        latent, latent_owner.reshape(1, GEN), next_owner.reshape(1, DSLOTS), cache_latent,
        cache_act, weight_in, bias_in, norm_gain, norm_shift, sel, rest,
    )
    return decode(*made, weight_in, bias_in, norm_gain, norm_shift, bias_mid, sel, rest, weight_mid)


def solution(mesh):
    both = ("gen", "dec")
    in_specs = (
        P(both, None, None), P(both, None), P(both), P(both, None, None), P(both, None, None),
        P(), P(), P(), P(), P(), P(),
    )
    out_specs = (P(both, None, None),) * 4
    return jax.shard_map(shards, mesh=mesh, in_specs=in_specs, out_specs=out_specs, check_vma=False)
```
